256 devices in a mesh: ctx: 64 (over z, x, core), head: 4 (over y).
Axes of the slice: x: 4, y: 4, z: 8, core: 2. Of those that a mesh axis runs over, the one named last changes fastest.
Arguments:
- query_plain: bfloat16 [4096, 64, 128], P('ctx', 'head'), may hold values from -6 to 6
- query_rotary: bfloat16 [4096, 64, 64], P('ctx', 'head'), may hold values from -480 to 480
- latent_cache: bfloat16 [4096, 512], P('ctx'), may hold values from -6 to 6
- key_rotary: bfloat16 [4096, 64], P('ctx'), may hold values from -4 to 4
- latent_gain: float32 [512], replicated, may hold values from 0.1 to 1.9
- positions: int32 [4096], P('ctx'), may hold values from 0 to 4095, as said below
- absorb_keys: bfloat16 [64, 128, 512], P('head'), may hold values from -0.5 to 0.5
- absorb_values: bfloat16 [64, 512, 128], P('head'), may hold values from -0.25 to 0.25
- output_weight: bfloat16 [64, 128, 3584], P('head', 'ctx'), may hold values from -0.0625 to 0.0625
Outputs:
- attention_out: bfloat16 [4096, 3584], P('ctx', 'head')
The draws below stay inside these ranges and needn't reach their ends.
Inputs may be any that keep to these rules, and one draw needn't show every extreme that they name: A permutation of the 4096 positions; the stored tokens come in aligned blocks of 32 rows, each block holding 32 consecutive positions in ascending order; the blocks stand in any order.
All inputs are finite; a program needn't handle non-finite values.
Results may differ from the reference program's by a relative error of at most 0.018.
The reference program's roundings to bfloat16 on the way count: a program that leaves them out, or rounds other values in their place, can miss the bound.
Values may be sent and summed in bfloat16 or wider, within the bound.
A program may use at most 128 MiB of HBM per device.

```python
import math
import jax
import jax.numpy as jnp
from jax import lax

HEADS = 64
NOPE = 128
ROPE = 64
LAT = 512
VD = 128
DW = 3584
TOKENS = 4096
GROUP = 32


def draw_key_rotary(key, part):
    key = jax.random.fold_in(key, 7)
    return jnp.clip(jax.random.normal(key, (TOKENS, ROPE), jnp.float32), -4.0, 4.0).astype(jnp.bfloat16)


def draw_query_rotary(key, part):
    key = jax.random.fold_in(key, 9)
    noise = jnp.clip(jax.random.normal(key, (TOKENS, HEADS, ROPE), jnp.float32), -4.0, 4.0)
    return noise.astype(jnp.bfloat16)


def draw_positions(key, part):
    key = jax.random.fold_in(key, 11)
    order = jax.random.permutation(key, TOKENS // GROUP).astype(jnp.int32)
    inside = jnp.arange(GROUP, dtype=jnp.int32)
    return (order[:, None] * GROUP + inside[None, :]).reshape(TOKENS).astype(jnp.int32)


def levels(stream_key, dims, shards, smallest, largest):
    loudness, own = 1.0, jax.random.fold_in(stream_key, 6)
    for dim, parts in shards:
        draws = jnp.exp(jax.random.uniform(jax.random.fold_in(own, dim), (parts,), jnp.float32, smallest / len(shards), largest / len(shards)))
        loudness = loudness * jnp.repeat(draws, dims[dim] // parts).reshape([-1 if axis == dim else 1 for axis in range(len(dims))])
    return loudness


def normal_values(own_key, dims, scale, limit, cuts=(), kind=jnp.bfloat16):
    result = jax.random.normal(own_key, dims, jnp.float32) * scale
    if len(cuts) > 0:
        result = levels(own_key, dims, cuts, -0.22, 0.18) * result
    return jnp.clip(result, min=-limit, max=limit).astype(kind)


def setup_inputs(seed: int = 0) -> dict:
    arg_keys = jax.random.split(jax.random.key(seed), 10)
    query_plain = normal_values(arg_keys[0], (TOKENS, HEADS, NOPE), 1.0, 6.0, ((0, 64), (1, 4)))
    query_rotary = draw_query_rotary(jax.random.fold_in(arg_keys[9], 71), 0)
    latent_cache = normal_values(arg_keys[2], (TOKENS, LAT), 1.0, 6.0, ((0, 64),))
    key_rotary = draw_key_rotary(jax.random.fold_in(arg_keys[9], 71), 0)
    latent_gain = jnp.clip(1.0 + 0.18 * jax.random.normal(arg_keys[4], (LAT,), jnp.float32), 0.1, 1.9)
    positions = draw_positions(jax.random.fold_in(arg_keys[9], 71), 0)
    absorb_keys = normal_values(arg_keys[6], (HEADS, NOPE, LAT), NOPE ** -0.5, 0.5, ((0, 4),))
    absorb_values = normal_values(arg_keys[7], (HEADS, LAT, VD), LAT ** -0.5, 0.25, ((0, 4),))
    output_weight = normal_values(arg_keys[8], (HEADS, VD, DW), (HEADS * VD) ** -0.5, 0.0625, ((0, 4), (1, 64)))
    return {"query_plain": query_plain, "query_rotary": query_rotary, "latent_cache": latent_cache, "key_rotary": key_rotary, "latent_gain": latent_gain, "positions": positions, "absorb_keys": absorb_keys, "absorb_values": absorb_values, "output_weight": output_weight}


norm_epsilon = 1e-06
rope_base = 10000.0
masked_score = -1e+30

def rotate(values, where_at):
    half_width = values.shape[-1] // 2
    frequency = rope_base ** (-jnp.arange(half_width, dtype=jnp.float32) / half_width)
    angles = where_at.astype(jnp.float32)[..., None] * frequency
    cosine_part = jnp.cos(angles)
    sine_part = jnp.sin(angles)
    first_half = values[..., :half_width]
    second_half = values[..., half_width:]
    return jnp.concatenate([first_half * cosine_part - second_half * sine_part, second_half * cosine_part + first_half * sine_part], axis=-1)

def reference(query_plain, query_rotary, latent_cache, key_rotary, latent_gain, positions, absorb_keys, absorb_values, output_weight):
    raw_latent = latent_cache.astype(jnp.float32)
    latent = (raw_latent * lax.rsqrt(lax.optimization_barrier(jnp.mean(raw_latent * raw_latent, axis=-1, keepdims=True)) + norm_epsilon) * latent_gain).astype(jnp.bfloat16)
    key_rot = rotate(key_rotary.astype(jnp.float32), positions).astype(jnp.bfloat16)
    keys = jnp.concatenate([latent, key_rot], axis=-1)
    query_abs = jnp.einsum('thn,hnl->thl', query_plain.astype(jnp.float32), absorb_keys.astype(jnp.float32)).astype(jnp.bfloat16)
    query_rot = rotate(query_rotary.astype(jnp.float32), positions[:, None]).astype(jnp.bfloat16)
    queries = jnp.concatenate([query_abs, query_rot], axis=-1)
    score_scale = (NOPE + ROPE) ** (-0.5)
    block_size = math.gcd(TOKENS, 256)
    block_count = TOKENS // block_size
    keys_wide = keys.astype(jnp.float32)
    latent_wide = latent.astype(jnp.float32)

    def attend(inputs):
        query_block, query_pos = inputs
        scores = jnp.einsum('thw,sw->ths', query_block.astype(jnp.float32), keys_wide) * score_scale
        visible = positions[None, None, :] <= query_pos[:, None, None]
        masked = jnp.where(visible, scores, masked_score)
        top_score = lax.optimization_barrier(jnp.max(masked, axis=-1, keepdims=True))
        expo = jnp.where(visible, jnp.exp(masked - top_score), 0.0)
        weight_sum = lax.optimization_barrier(jnp.sum(expo, axis=-1))
        weights = expo.astype(jnp.bfloat16).astype(jnp.float32)
        context_sum = jnp.einsum('ths,sl->thl', weights, latent_wide)
        return (context_sum / weight_sum[..., None]).astype(jnp.bfloat16)
    context = lax.map(attend, (queries.reshape(block_count, block_size, HEADS, LAT + ROPE), positions.reshape(block_count, block_size)))
    context = context.reshape(TOKENS, HEADS, LAT)
    head_out = jnp.einsum('thl,hlv->thv', context.astype(jnp.float32), absorb_values.astype(jnp.float32)).astype(jnp.bfloat16)
    summed = jnp.einsum('thv,hvd->td', head_out.astype(jnp.float32), output_weight.astype(jnp.float32))
    return summed.astype(jnp.bfloat16)
```

```python
import jax
import jax.numpy as jnp
from jax import lax
from jax.experimental import pallas as pl
from jax.experimental.pallas import tpu as pltpu
from jax.sharding import PartitionSpec as P

MESH = pl.DeviceIdType.MESH
norm_epsilon = 1e-06
rope_base = 10000.0
masked_score = -1e30

NZ, NX, NY = 8, 4, 4
TOK = 64
HALF = 32
HEADS = 16
ROWS = TOK * HEADS
NOPE, ROPE, LAT, VD = 128, 64, 512, 128
COLS = 896
CHUNK = 256
CHUNKS = ROWS // CHUNK
WIDE = 2 * LAT + 2 * ROPE
SCALE = 192 ** (-0.5)
LOG2E = 1.4426950408889634

SLOTS = [
    "own", "R1", "L1", "Dm0", "Dp0", "R2", "L2", "Do0",
    "R3", "L3", "Ym", "Yp", "R4", "Yo", "Dm3", "Dp3",
    "Em", "Ep", "Amm", "Apm", "Amp", "App", "Amo", "Apo",
    "Fm", "Fp", "Do3", "Eo", "Aom", "Aop", "Aoo", "Fo",
]
SLOT = {name: i for i, name in enumerate(SLOTS)}

FORWARD = {
    "own": [("z+", "R1"), ("z-", "L1"), ("x+", "Dm0"), ("x-", "Dp0")],
    "R1": [("z+", "R2")],
    "R2": [("z+", "R3")],
    "R3": [("z+", "R4"), ("x+", "Dm3"), ("x-", "Dp3")],
    "L1": [("z-", "L2")],
    "L2": [("z-", "L3")],
    "L3": [("x+", "Em"), ("x-", "Ep")],
    "R4": [("x+", "Fm"), ("x-", "Fp")],
    "Dm0": [("x+", "Do0")],
    "Dp3": [("x-", "Do3")],
    "Em": [("x+", "Eo")],
    "Fp": [("x-", "Fo")],
    "Ym": [("x+", "Yo"), ("y+", "Amm"), ("y-", "Apm")],
    "Yp": [("y+", "Amp"), ("y-", "App")],
    "Yo": [("y+", "Amo"), ("y-", "Apo")],
    "Amm": [("y+", "Aom")],
    "App": [("y-", "Aop")],
    "Amo": [("y+", "Aoo")],
}
SHARED = {"R1": 0, "L1": 1, "R2": 2, "L2": 3}

XD = {"m": 3, "p": 1, "o": 2}


def origin(name):
    if name == "own":
        return 0, 0
    if name[0] == "R":
        return 0, NZ - int(name[1])
    if name[0] == "L":
        return 0, int(name[1])
    if name[0] == "D":
        return XD[name[1]], (0 if name[2] == "0" else NZ - 3)
    if name[0] == "E":
        return XD[name[1]], 3
    if name[0] == "F":
        return XD[name[1]], 4
    if name[0] == "Y":
        return XD[name[1]], ("y", 0)
    return XD[name[2]], ("y", XD[name[1]])


def kernel(
    qp_ref, qr_ref, lat_ref, kr_ref, gain_ref, pos_ref, cos_ref, sin_ref, ak_hbm, av_hbm, w_ref,
    out_ref,
    ak, av, kx, qh, q2, s_buf, top, kpos, psrc, pline, pall, wp, wf, ctx_acc, ho, acc, outs, rcv,
    local_sem, key_send, key_recv, sib_send, sib_recv, p_send, p_recv, w1_send, w1_recv,
    w2_send, w2_recv, w3_send, w3_recv, ho_send, ho_recv, out_send, out_recv,
):
    f32, bf16 = jnp.float32, jnp.bfloat16
    me = lax.axis_index("ctx")
    y = lax.axis_index("head")
    core = lax.rem(me, 2)
    x = lax.rem(me // 2, NX)
    z = me // (2 * NX)

    def device(dz=0, dx=0, dc=0, dy=0):
        nz = lax.rem(z + (dz + NZ), NZ)
        nx = lax.rem(x + (dx + NX), NX)
        nc = lax.rem(core + dc, 2)
        ny = lax.rem(y + (dy + NY), NY)
        return ((nz * NX + nx) * 2 + nc, ny)

    sibling = device(dc=1)
    where = {
        "z+": device(dz=1), "z-": device(dz=-1), "x+": device(dx=1), "x-": device(dx=-1),
        "y+": device(dy=1), "y-": device(dy=-1),
    }
    column_peers = [device(dz=d) for d in range(1, NZ)]
    chip_peers = [(dx, dc) for dx in range(NX) for dc in range(2) if (dx, dc) != (0, 0)]
    plane_peers = [device(dx=dx, dy=dy) for dx in range(NX) for dy in range(1, NY)]
    partners = column_peers + [device(dx=a, dc=b) for a, b in chip_peers] + plane_peers

    barrier = pltpu.get_barrier_semaphore()
    for partner in partners:
        pl.semaphore_signal(barrier, inc=1, device_id=partner, device_id_type=MESH)

    load_ak = pltpu.make_async_copy(ak_hbm, ak, local_sem.at[0])
    load_av = pltpu.make_async_copy(av_hbm, av, local_sem.at[1])
    load_ak.start()
    load_av.start()

    def remote(src, dst, send, recv, to):
        return pltpu.make_async_remote_copy(
            src_ref=src, dst_ref=dst, send_sem=send, recv_sem=recv, device_id=to, device_id_type=MESH
        )

    def dot(a, b):
        return jnp.dot(a, b, preferred_element_type=f32)

    def iota(shape, axis):
        return lax.broadcasted_iota(jnp.int32, shape, axis)

    def onehot(mask):
        return jnp.where(mask, 1.0, 0.0).astype(bf16)

    def slot_ref(p, sib=0):
        return kx.at[2 * (p // 8) + sib, pl.ds((p % 8) * HALF, HALF), :]

    pending = []

    def send_block(p, to, dst):
        index = len(pending)
        copy = remote(slot_ref(p), slot_ref(dst), key_send.at[index], key_recv.at[dst], to)
        copy.start()
        pending.append(copy)

    def to_sibling(p):
        remote(slot_ref(p), slot_ref(p, 1), sib_send.at[p], sib_recv.at[p], sibling).start()

    def filled(name):
        p = SLOT[name]
        for direction, dst in FORWARD.get(name, []):
            send_block(p, where[direction], SLOT[dst])
        to_sibling(p)
        if name in SHARED:

            @pl.when(y == SHARED[name])
            def _():
                for k, (direction, dst) in enumerate((("x+", "Ym"), ("x-", "Yp"))):
                    remote(
                        slot_ref(p), slot_ref(SLOT[dst]), key_send.at[60 + k],
                        key_recv.at[SLOT[dst]], where[direction],
                    ).start()

    def arrived(name):
        p = SLOT[name]
        remote(slot_ref(p), slot_ref(p), key_send.at[0], key_recv.at[p], sibling).wait_recv()
        filled(name)

    raw = lat_ref[...].astype(f32)
    spread = jnp.sum(raw * raw, axis=-1, keepdims=True) * (1.0 / LAT)
    latent = (raw * lax.rsqrt(spread + norm_epsilon) * gain_ref[...]).astype(bf16)
    row_i, col_i = iota((ROPE, 128), 0), iota((ROPE, 128), 1)
    low = iota((HALF, 128), 1) < ROPE
    kr = kr_ref[...]
    first = onehot(col_i == row_i)
    second = onehot(col_i == row_i + ROPE)
    turned = (row_i + HALF) & (ROPE - 1)
    first_turned = onehot(col_i == turned)
    second_turned = onehot(col_i == turned + ROPE)
    straight = dot(kr[:HALF], first) + dot(kr[HALF:], second)
    crossed = dot(kr[:HALF], first_turned) + dot(kr[HALF:], second_turned)
    cosine, sine = cos_ref[...], sin_ref[...]
    key_rot = straight * jnp.where(low, cosine[:HALF], cosine[HALF:]) + crossed * jnp.where(
        low, sine[:HALF], sine[HALF:]
    )
    kx[0, 0:HALF, 0:LAT] = latent[:HALF]
    kx[0, 0:HALF, LAT : LAT + 128] = key_rot.astype(bf16)
    kx[0, 0:HALF, LAT + 128 : WIDE] = latent[HALF:]
    lane = iota((8, 2 * CHUNK), 1)
    base = jnp.where(lane < CHUNK, pos_ref[0:1, 0:1], pos_ref[HALF : HALF + 1, 0:1])
    psrc[...] = base + (lane & (HALF - 1)).astype(f32)

    pl.semaphore_wait(barrier, len(partners))

    filled("own")
    column_sends = []
    for d in range(1, NZ):
        copy = remote(psrc, pline.at[NZ - d], p_send.at[d], p_recv.at[NZ - d], column_peers[d - 1])
        copy.start()
        column_sends.append(copy)

    def weight_piece(nx, nc):
        return w_ref.at[
            pl.ds(pl.multiple_of(nc * 16, 16), 16), pl.ds(pl.multiple_of(nx * COLS, 128), COLS)
        ]

    my_place = x * 2 + core
    weight_sends = []
    for k, (dx, dc) in enumerate(chip_peers):
        nx, nc = lax.rem(x + dx, NX), lax.rem(core + dc, 2)
        copy = remote(
            weight_piece(nx, nc), wp.at[my_place], w1_send.at[k], w1_recv.at[my_place],
            device(dx=dx, dc=dc),
        )
        copy.start()
        weight_sends.append(copy)
    own_weight = pltpu.make_async_copy(weight_piece(x, core), wp.at[my_place], local_sem.at[2])
    own_weight.start()

    big_i, big_j = iota((256, 256), 0), iota((256, 256), 1)
    swap = onehot(big_j == ((big_i & 15) << 4) + (big_i >> 4))
    doubled = jnp.concatenate(
        [first + second, first_turned + second_turned], axis=1
    )
    low_q = iota((256, 128), 1) < ROPE
    for b in range(TOK // 16):
        rows = slice(b * 256, (b + 1) * 256)
        plain = dot(swap, qp_ref[rows, :]).astype(bf16).reshape(HEADS, 16, NOPE)
        qh[:, b * 16 : (b + 1) * 16, :] = plain
        both = dot(swap, dot(qr_ref[rows, :], doubled).astype(bf16))
        tokens = slice(b * 16, (b + 1) * 16)
        c_rows = jnp.concatenate([cosine[tokens]] * HEADS, axis=0)
        s_rows = jnp.concatenate([sine[tokens]] * HEADS, axis=0)
        turned_q = both[:, :128] * c_rows + both[:, 128:] * s_rows
        q_first = jnp.where(low_q, turned_q, 0.0).astype(bf16).reshape(HEADS, 16, 128)
        q_second = jnp.where(low_q, 0.0, turned_q).astype(bf16).reshape(HEADS, 16, 128)
        q2[:, b * 16 : (b + 1) * 16, 0:128] = q_second
        q2[:, b * 16 : (b + 1) * 16, 128 + LAT :] = q_first

    arrived("R1")
    arrived("L1")
    arrived("Dm0")
    arrived("Dp0")
    load_ak.wait()

    def absorb(h, carry):
        q2[h, :, 128 : 128 + LAT] = dot(qh[h], ak[h]).astype(bf16)
        return carry

    lax.fori_loop(0, HEADS // 2, absorb, 0)
    arrived("R2")
    arrived("L2")
    arrived("Do0")
    lax.fori_loop(HEADS // 2, HEADS, absorb, 0)

    for d in range(1, NZ):
        remote(psrc, pline.at[d], p_send.at[d], p_recv.at[d], sibling).wait_recv()
    line = psrc[...]
    which = iota((8, 2 * CHUNK), 0)
    for d in range(1, NZ):
        line = jnp.where(which == d, pline[d], line)
    pall[0] = line
    line_sends = []
    for k, (dx, dc) in enumerate(chip_peers):
        there = ((NX - dx) % NX) * 2 + dc
        copy = remote(
            pall.at[0], pall.at[there], p_send.at[8 + k], p_recv.at[8 + there], device(dx=dx, dc=dc)
        )
        copy.start()
        line_sends.append(copy)

    arrived("R3")
    arrived("L3")
    arrived("Ym")
    arrived("Yp")
    for k, (dx, dc) in enumerate(chip_peers):
        here = dx * 2 + dc
        remote(pall.at[0], pall.at[here], p_send.at[0], p_recv.at[8 + here], sibling).wait_recv()

    def shared_offset(dy):
        owner = lax.rem(y + dy, NY)
        far, sign = 1 + owner // 2, lax.rem(owner, 2) * 2 - 1
        return lax.rem(far * sign + NZ, NZ)

    group = (iota((1, 2 * CHUNK), 1) & (CHUNK - 1)) >> 5
    for tile in range(8):
        stage, dc = tile // 2, tile % 2
        value = jnp.zeros((1, 2 * CHUNK), f32)
        for q in range(8):
            dx, dz = origin(SLOTS[stage * 8 + q])
            if isinstance(dz, tuple):
                dz = shared_offset(dz[1])
            value = jnp.where(group == q, pall[dx * 2 + dc, pl.ds(dz, 1), :], value)
        kpos[tile, 0:1, :] = value

    query_pos = jnp.concatenate([pos_ref[:, 0:1]] * (CHUNK // TOK), axis=0)
    top[...] = jnp.full(top.shape, masked_score, f32)
    contract = (((1,), (1,)), ((), ()))
    chunk_heads = CHUNK // TOK

    def scores(tile):
        def one(r, carry):
            heads = pl.ds(r * chunk_heads, chunk_heads)
            rows = pl.ds(pl.multiple_of(r * CHUNK, CHUNK), CHUNK)
            q_a = q2[heads, :, 128:].reshape(CHUNK, LAT + 128)
            q_b = q2[heads, :, 0 : LAT + 128].reshape(CHUNK, LAT + 128)
            best = top[rows, :]
            for part, (q, k) in enumerate(
                ((q_a, kx[tile, :, 0 : LAT + 128]), (q_b, kx[tile, :, LAT:WIDE]))
            ):
                s = lax.dot_general(q, k, contract, preferred_element_type=f32)
                lanes = slice(part * CHUNK, (part + 1) * CHUNK)
                s = jnp.where(kpos[tile, 0:1, lanes] <= query_pos, s, masked_score)
                s_buf[tile, rows, lanes] = s
                best = jnp.maximum(best, jnp.maximum(s[:, :128], s[:, 128:]))
            top[rows, :] = best
            return carry

        lax.fori_loop(0, CHUNKS, one, 0)

    def from_sibling(stage):
        for p in range(stage * 8, stage * 8 + 8):
            remote(
                slot_ref(p, 1), slot_ref(p, 1), sib_send.at[p], sib_recv.at[p], sibling
            ).wait_recv()

    scores(0)
    arrived("R4")
    arrived("Yo")

    for k, (dx, dc) in enumerate(chip_peers):
        place = lax.rem(x + dx, NX) * 2 + lax.rem(core + dc, 2)
        remote(wp.at[place], wp.at[place], w1_send.at[0], w1_recv.at[place], sibling).wait_recv()
    own_weight.wait()
    to_i, from_i = iota((128, 128), 0), iota((128, 128), 1)
    regroup = onehot(
        from_i == (((to_i & 15) >> 1) << 4) + ((to_i >> 4) << 1) + (to_i & 1)
    )
    share = dot(regroup, wp[...].reshape(128, COLS)).astype(bf16).reshape(8, 16, COLS)

    def weight_slot(dz, half):
        nz = lax.rem(z + (dz + NZ), NZ)
        return wf.at[
            pl.ds(core * 8 + half * 4, 4), pl.ds(pl.multiple_of(nz * 16, 16), 16), :
        ]

    wf[pl.ds(core * 8, 8), pl.ds(pl.multiple_of(z * 16, 16), 16), :] = share
    ring_sends = []

    def weight_on(dz, half):
        index = (dz % NZ) * 2 + half
        here = weight_slot(dz, half)
        copy = remote(here, here, w3_send.at[index], w3_recv.at[index], sibling)
        copy.start()
        ring_sends.append(copy)
        steps = []
        if -3 < dz <= 0 or (dz == -3 and half == 0):
            steps.append(("z+", dz - 1))
        if 0 <= dz < 3 or (dz == 3 and half == 1):
            steps.append(("z-", dz + 1))
        for direction, there in steps:
            arrival = (there % NZ) * 2 + half
            copy = remote(
                here, here, w2_send.at[len(ring_sends) - 1], w2_recv.at[arrival], where[direction]
            )
            copy.start()
            ring_sends.append(copy)

    def weight_arrived(dz, half):
        index = (dz % NZ) * 2 + half
        here = weight_slot(dz, half)
        remote(here, here, w2_send.at[0], w2_recv.at[index], sibling).wait_recv()
        weight_on(dz, half)

    def weight_step(step):
        for half in range(2):
            if step < 4:
                weight_arrived(-step, half)
                weight_arrived(step, half)
            else:
                weight_arrived(-4 if half == 0 else 4, half)

    weight_on(0, 0)
    weight_on(0, 1)

    arrived("Dm3")
    arrived("Dp3")
    from_sibling(0)
    scores(1)
    for name in SLOTS[16:20]:
        arrived(name)
    scores(2)
    for name in SLOTS[20:24]:
        arrived(name)
    from_sibling(1)
    scores(3)
    weight_step(1)
    for name in SLOTS[24:28]:
        arrived(name)
    scores(4)
    for name in SLOTS[28:32]:
        arrived(name)
    from_sibling(2)
    scores(5)
    scores(6)
    from_sibling(3)
    scores(7)
    weight_step(2)

    load_av.wait()
    factor = SCALE * LOG2E
    exchange = []

    def head_out_send(c, to, place, index):
        piece = ho.at[c, place]
        copy = remote(piece, piece, ho_send.at[index], ho_recv.at[index], to)
        copy.start()
        exchange.append(copy)

    def head_out_wait(c, dx):
        place = lax.rem(x + dx, NX)
        index = c * 3 + (dx - 1)
        piece = ho.at[c, place]
        remote(piece, piece, ho_send.at[0], ho_recv.at[index], sibling).wait_recv()
        return place

    def head_out_forward(c):
        place = head_out_wait(c, 3)
        if c % 2 == 0:
            head_out_send(c, where["x+"], place, c * 3 + 1)
        place = head_out_wait(c, 1)
        if c % 2 == 1:
            head_out_send(c, where["x-"], place, c * 3 + 1)

    for c in range(CHUNKS):
        rows = slice(c * CHUNK, (c + 1) * CHUNK)
        peak = jnp.max(top[rows, :], axis=1, keepdims=True)
        ctx_acc[...] = jnp.zeros(ctx_acc.shape, f32)

        def one(tile, total, rows=rows, peak=peak):
            grown = jnp.zeros((CHUNK, LAT), f32)
            for part, cols in enumerate((slice(0, LAT), slice(LAT + 128, WIDE))):
                lanes = slice(part * CHUNK, (part + 1) * CHUNK)
                expo = jnp.exp2((s_buf[tile, rows, lanes] - peak) * factor)
                total = total + expo[:, :128] + expo[:, 128:]
                grown = grown + dot(expo.astype(bf16), kx[tile, :, cols])
            ctx_acc[...] += grown
            return total

        total = lax.fori_loop(0, 8, one, jnp.zeros((CHUNK, 128), f32))
        total = jnp.sum(total, axis=1, keepdims=True)
        context = (ctx_acc[...] / total).astype(bf16)
        for k in range(chunk_heads):
            head = c * chunk_heads + k
            value = dot(context[k * TOK : (k + 1) * TOK], av[head])
            ho[c, x, :, k * VD : (k + 1) * VD] = value.astype(bf16)
        head_out_send(c, where["x+"], x, c * 3 + 2)
        head_out_send(c, where["x-"], x, c * 3 + 0)
        if c > 0:
            head_out_forward(c - 1)
        if c == 1:
            weight_step(3)
    head_out_forward(CHUNKS - 1)
    weight_step(4)
    for dz in range(NZ):
        for half in range(2):
            index = dz * 2 + half
            nz = lax.rem(z + dz, NZ)
            there = wf.at[
                pl.ds((1 - core) * 8 + half * 4, 4), pl.ds(pl.multiple_of(nz * 16, 16), 16), :
            ]
            remote(there, there, w3_send.at[0], w3_recv.at[index], sibling).wait_recv()

    for c in range(CHUNKS):
        head_out_wait(c, 2)
        part = dot(
            ho[c].reshape(NX * TOK, chunk_heads * VD),
            wf[c * chunk_heads : (c + 1) * chunk_heads].reshape(chunk_heads * VD, COLS),
        )
        if c == 0:
            acc[...] = part
        else:
            acc[...] += part
    outs[...] = acc[...].astype(bf16).reshape(NX, TOK, COLS)

    def result_copy(nx):
        return remote(
            outs.at[nx], rcv.at[y], out_send.at[nx], out_recv.at[y], ((z * NX + nx) * 2 + core, x)
        )

    for dx in range(NX):
        nx = lax.rem(x + dx, NX)
        if dx == 0:
            here = x == y

            @pl.when(here)
            def _():
                pltpu.make_async_copy(outs.at[nx], rcv.at[y], out_recv.at[y]).start()

            @pl.when(jnp.logical_not(here))
            def _():
                result_copy(nx).start()
        else:
            result_copy(nx).start()
    final = jnp.zeros((TOK, COLS), f32)
    for k in range(NY):
        pltpu.make_async_copy(rcv.at[k], rcv.at[k], out_recv.at[k]).wait()
        final = final + rcv[k].astype(f32)
    out_ref[...] = final.astype(bf16)

    for dx in range(NX):
        nx = lax.rem(x + dx, NX)
        if dx == 0:

            @pl.when(x != y)
            def _():
                result_copy(nx).wait_send()
        else:
            result_copy(nx).wait_send()
    for copy in pending + column_sends + weight_sends + line_sends + ring_sends + exchange:
        copy.wait_send()
    for k in range(2):
        remote(slot_ref(0), slot_ref(0), key_send.at[60 + k], key_recv.at[0], sibling).wait_send()
    for p in range(32):
        remote(slot_ref(p), slot_ref(p), sib_send.at[p], sib_recv.at[p], sibling).wait_send()


def body(
    query_plain,
    query_rotary,
    latent_cache,
    key_rotary,
    latent_gain,
    positions,
    absorb_keys,
    absorb_values,
    output_weight,
):
    f32, bf16 = jnp.float32, jnp.bfloat16
    place = positions.astype(f32)
    pos = jnp.broadcast_to(place[:, None], (TOK, 128))
    half = ROPE // 2
    frequency = rope_base ** (-jnp.arange(half, dtype=f32) / half)
    angles = place[:, None] * jnp.tile(frequency, 4)[None, :]
    sign = jnp.where((jnp.arange(128) & (ROPE - 1)) < half, -1.0, 1.0).astype(f32)
    cosine = jnp.cos(angles)
    sine = jnp.sin(angles) * sign[None, :]
    vmem = pl.BlockSpec(memory_space=pltpu.VMEM)
    hbm = pl.BlockSpec(memory_space=pl.ANY)
    dma = pltpu.SemaphoreType.DMA
    call = pl.pallas_call(
        kernel,
        out_shape=jax.ShapeDtypeStruct((TOK, COLS), bf16),
        in_specs=[vmem] * 8 + [hbm] * 2 + [vmem],
        out_specs=vmem,
        scratch_shapes=[
            pltpu.VMEM((HEADS, NOPE, LAT), bf16),
            pltpu.VMEM((HEADS, LAT, VD), bf16),
            pltpu.VMEM((8, 8 * HALF, WIDE), bf16),
            pltpu.VMEM((HEADS, TOK, NOPE), bf16),
            pltpu.VMEM((HEADS, TOK, LAT + 256), bf16),
            pltpu.VMEM((8, ROWS, 2 * CHUNK), f32),
            pltpu.VMEM((ROWS, 128), f32),
            pltpu.VMEM((8, 8, 2 * CHUNK), f32),
            pltpu.VMEM((8, 2 * CHUNK), f32),
            pltpu.VMEM((NZ, 8, 2 * CHUNK), f32),
            pltpu.VMEM((8, 8, 2 * CHUNK), f32),
            pltpu.VMEM((8, 16, COLS), bf16),
            pltpu.VMEM((HEADS, VD, COLS), bf16),
            pltpu.VMEM((CHUNK, LAT), f32),
            pltpu.VMEM((CHUNKS, NX, TOK, CHUNK // TOK * VD), bf16),
            pltpu.VMEM((NX * TOK, COLS), f32),
            pltpu.VMEM((NX, TOK, COLS), bf16),
            pltpu.VMEM((NY, TOK, COLS), bf16),
            dma((3,)),
            dma((62,)),
            dma((32,)),
            dma((32,)),
            dma((32,)),
            dma((16,)),
            dma((16,)),
            dma((8,)),
            dma((8,)),
            dma((32,)),
            dma((16,)),
            dma((16,)),
            dma((16,)),
            dma((12,)),
            dma((12,)),
            dma((4,)),
            dma((4,)),
        ],
        compiler_params=pltpu.CompilerParams(
            collective_id=0, has_side_effects=True, vmem_limit_bytes=60 * 1024 * 1024
        ),
        cost_estimate=pl.CostEstimate(
            flops=11_000_000_000, bytes_accessed=6_000_000, transcendentals=4_200_000
        ),
    )
    return call(
        query_plain.reshape(ROWS, NOPE),
        query_rotary.reshape(ROWS, ROPE),
        latent_cache,
        key_rotary,
        latent_gain.reshape(1, LAT),
        pos,
        cosine,
        sine,
        absorb_keys,
        absorb_values,
        output_weight.reshape(2 * HEADS, -1),
    )


def solution(mesh):
    return jax.shard_map(
        body,
        mesh=mesh,
        in_specs=(
            P("ctx", "head", None),
            P("ctx", "head", None),
            P("ctx", None),
            P("ctx", None),
            P(),
            P("ctx"),
            P("head", None, None),
            P("head", None, None),
            P("head", "ctx", None),
        ),
        out_specs=P("ctx", "head"),
        check_vma=False,
    )
```

```python
import jax
import jax.numpy as jnp
import numpy as np
from jax import lax
from jax.experimental import pallas as pl
from jax.experimental.pallas import tpu as pltpu
from jax.sharding import PartitionSpec as P

MESH = pl.DeviceIdType.MESH
norm_epsilon = 1e-06
rope_base = 10000.0
masked_score = -1e30

NZ, NX, NY = 8, 4, 4
TOK = 64
HALF = 32
HEADS = 16
ROWS = TOK * HEADS
NOPE, ROPE, LAT, VD = 128, 64, 512, 128
COLS = 896
KEYS = 2 * LAT + 2 * ROPE
WIDE = KEYS + 128
SCALE = 192 ** (-0.5)
LOG2E = 1.4426950408889634

SLOTS = [
    "own", "R1", "L1", "m0", "p0", "R2", "L2", "o0",
    "Ym", "Yp", "Yo", "R3", "L3", "R4", "mR3", "pR3",
    "Amm", "Apm", "Amp", "App", "Aom", "Aop", "Amo", "Apo",
    "Aoo", "oR3", "mL3", "pL3", "oL3", "mR4", "pR4", "oR4",
]
SLOT = {name: i for i, name in enumerate(SLOTS)}


def along_x(name):
    return [("x+", "m" + name), ("x-", "p" + name), ("xx", "o" + name)]


def along_y(name):
    return [("y+", "Am" + name), ("y-", "Ap" + name), ("yy", "Ao" + name)]


FORWARD = {
    "own": [("z+", "R1"), ("z-", "L1"), ("z++", "R2"), ("z--", "L2"), ("x+", "m0"), ("x-", "p0")],
    "m0": [("x+", "o0")],
    "R2": [("z+", "R3"), ("z++", "R4")],
    "L2": [("z-", "L3")],
    "R3": along_x("R3"),
    "L3": along_x("L3"),
    "R4": along_x("R4"),
    "Ym": along_y("m"),
    "Yp": along_y("p"),
    "Yo": along_y("o"),
}
SHARED = {"R1": 0, "L1": 1, "R2": 2, "L2": 3}
SHARED_TO = (("x+", "Ym"), ("x-", "Yp"), ("xx", "Yo"))


def kernel(
    pos_ref, qp_ref, qr_ref, lat_ref, kr_ref, gain_ref, cos_g, sin_g, cos_i, sin_i, ak_hbm, av_hbm, w_ref,
    out_ref,
    ak, av, kx, qh, q2, s_buf, top, wp, wf, ho, outs, rcv,
    local_sem, key_send, key_recv, sib_send, sib_recv, w1_send, w1_recv,
    w2_send, w2_recv, w3_send, w3_recv, ho_send, ho_recv, out_send, out_recv,
):
    f32, bf16 = jnp.float32, jnp.bfloat16
    me = lax.axis_index("ctx")
    y = lax.axis_index("head")
    core = lax.rem(me, 2)
    x = lax.rem(me // 2, NX)
    z = me // (2 * NX)

    def device(dz=0, dx=0, dc=0, dy=0):
        nz = lax.rem(z + (dz + NZ), NZ)
        nx = lax.rem(x + (dx + NX), NX)
        nc = lax.rem(core + dc, 2)
        ny = lax.rem(y + (dy + NY), NY)
        return ((nz * NX + nx) * 2 + nc, ny)

    sibling = device(dc=1)
    where = {
        "z+": device(dz=1), "z-": device(dz=-1), "x+": device(dx=1), "x-": device(dx=-1),
        "y+": device(dy=1), "y-": device(dy=-1),
        "z++": device(dz=2), "z--": device(dz=-2), "xx": device(dx=2), "yy": device(dy=2),
    }
    column_peers = [device(dz=d) for d in range(1, NZ)]
    chip_peers = [(dx, dc) for dx in range(NX) for dc in range(2) if (dx, dc) != (0, 0)]
    plane_peers = [device(dx=dx, dy=dy) for dx in range(NX) for dy in range(1, NY)]
    partners = column_peers + [device(dx=a, dc=b) for a, b in chip_peers] + plane_peers

    barrier = pltpu.get_barrier_semaphore()
    for partner in partners:
        pl.semaphore_signal(barrier, inc=1, device_id=partner, device_id_type=MESH)

    load_ak = pltpu.make_async_copy(ak_hbm, ak, local_sem.at[0])
    load_av = pltpu.make_async_copy(av_hbm, av, local_sem.at[1])
    load_ak.start()
    load_av.start()

    def remote(src, dst, send, recv, to):
        return pltpu.make_async_remote_copy(
            src_ref=src, dst_ref=dst, send_sem=send, recv_sem=recv, device_id=to, device_id_type=MESH
        )

    def dot(a, b):
        return jnp.dot(a, b, preferred_element_type=f32)

    def iota(shape, axis):
        return lax.broadcasted_iota(jnp.int32, shape, axis)

    def onehot(mask):
        return jnp.where(mask, 1.0, 0.0).astype(bf16)

    def slot_ref(p, sib=0):
        return kx.at[2 * (p // 8) + sib, pl.ds((p % 8) * HALF, HALF), :]

    pending = []

    def send_block(p, to, dst):
        index = len(pending)
        copy = remote(slot_ref(p), slot_ref(dst), key_send.at[index], key_recv.at[dst], to)
        copy.start()
        pending.append(copy)

    def to_sibling(p):
        remote(slot_ref(p), slot_ref(p, 1), sib_send.at[p], sib_recv.at[p], sibling).start()

    def filled(name):
        p = SLOT[name]
        for direction, dst in FORWARD.get(name, []):
            send_block(p, where[direction], SLOT[dst])
        to_sibling(p)
        if name in SHARED:

            @pl.when(y == SHARED[name])
            def _():
                for k, (direction, dst) in enumerate(SHARED_TO):
                    remote(
                        slot_ref(p), slot_ref(SLOT[dst]), key_send.at[60 + k],
                        key_recv.at[SLOT[dst]], where[direction],
                    ).start()

    def arrived(name):
        p = SLOT[name]
        remote(slot_ref(p), slot_ref(p), key_send.at[0], key_recv.at[p], sibling).wait_recv()
        filled(name)

    raw = lat_ref[...].astype(f32)
    spread = jnp.sum(raw * raw, axis=-1, keepdims=True) * (1.0 / LAT)
    latent = (raw * lax.rsqrt(spread + norm_epsilon) * gain_ref[...]).astype(bf16)
    row_i, col_i = iota((ROPE, 128), 0), iota((ROPE, 128), 1)
    low = iota((HALF, 128), 1) < ROPE
    kr = kr_ref[...]
    first = onehot(col_i == row_i)
    second = onehot(col_i == row_i + ROPE)
    turned = (row_i + HALF) & (ROPE - 1)
    first_turned = onehot(col_i == turned)
    second_turned = onehot(col_i == turned + ROPE)
    straight = dot(kr[:HALF], first) + dot(kr[HALF:], second)
    crossed = dot(kr[:HALF], first_turned) + dot(kr[HALF:], second_turned)
    groups = [pos_ref[0] >> 5, pos_ref[HALF] >> 5]
    cosines, sines = [], []
    for g in groups:
        c_g, s_g = cos_g[pl.ds(g, 1), :], sin_g[pl.ds(g, 1), :]
        cosines.append(c_g * cos_i[...] - s_g * sin_i[...])
        sines.append(s_g * cos_i[...] + c_g * sin_i[...])
    minus = jnp.where((iota((TOK, 128), 1) & (ROPE - 1)) < HALF, -1.0, 1.0)
    cosine = jnp.concatenate(cosines, axis=0)
    sine = jnp.concatenate(sines, axis=0) * minus
    key_rot = straight * jnp.where(low, cosine[:HALF], cosine[HALF:]) + crossed * jnp.where(
        low, sine[:HALF], sine[HALF:]
    )
    lane = iota((HALF, 128), 1)
    marks = jnp.where(
        lane == 0, groups[0].astype(f32), jnp.where(lane == 1, groups[1].astype(f32), 0.0)
    )
    kx[0, 0:HALF, 0:LAT] = latent[:HALF]
    kx[0, 0:HALF, LAT : LAT + 128] = key_rot.astype(bf16)
    kx[0, 0:HALF, LAT + 128 : KEYS] = latent[HALF:]
    kx[0, 0:HALF, KEYS:WIDE] = marks.astype(bf16)

    big_i, big_j = iota((256, 256), 0), iota((256, 256), 1)
    swap = onehot(big_j == ((big_i & 15) << 4) + (big_i >> 4))
    doubled = jnp.concatenate(
        [first + second, first_turned + second_turned], axis=1
    )
    low_q = iota((256, 128), 1) < ROPE
    for b in range(TOK // 16):
        rows = slice(b * 256, (b + 1) * 256)
        plain = dot(swap, qp_ref[rows, :]).astype(bf16).reshape(HEADS, 16, NOPE)
        qh[:, b * 16 : (b + 1) * 16, :] = plain
        both = dot(swap, dot(qr_ref[rows, :], doubled).astype(bf16))
        tokens = slice(b * 16, (b + 1) * 16)
        c_rows = jnp.concatenate([cosine[tokens]] * HEADS, axis=0)
        s_rows = jnp.concatenate([sine[tokens]] * HEADS, axis=0)
        turned_q = both[:, :128] * c_rows + both[:, 128:] * s_rows
        q_first = jnp.where(low_q, turned_q, 0.0).astype(bf16).reshape(HEADS, 16, 128)
        q_second = jnp.where(low_q, 0.0, turned_q).astype(bf16).reshape(HEADS, 16, 128)
        there = slice((b % 2) * 16, (b % 2) * 16 + 16)
        q2[b // 2, :, there, 0:128] = q_second
        q2[b // 2, :, there, 128 + LAT :] = q_first
    load_ak.wait()
    for h in range(HEADS):
        absorbed = dot(qh[h], ak[h]).astype(bf16)
        q2[0, h, :, 128 : 128 + LAT] = absorbed[:HALF]
        q2[1, h, :, 128 : 128 + LAT] = absorbed[HALF:]

    pl.semaphore_wait(barrier, len(partners))

    filled("own")

    def weight_piece(nx, nc):
        return w_ref.at[
            pl.ds(pl.multiple_of(nc * 16, 16), 16), pl.ds(pl.multiple_of(nx * COLS, 128), COLS)
        ]

    my_place = x * 2 + core
    weight_sends = []
    for k, (dx, dc) in enumerate(chip_peers):
        nx, nc = lax.rem(x + dx, NX), lax.rem(core + dc, 2)
        copy = remote(
            weight_piece(nx, nc), wp.at[my_place], w1_send.at[k], w1_recv.at[my_place],
            device(dx=dx, dc=dc),
        )
        copy.start()
        weight_sends.append(copy)
    own_weight = pltpu.make_async_copy(weight_piece(x, core), wp.at[my_place], local_sem.at[2])
    own_weight.start()

    for name in SLOTS[1:14]:
        arrived(name)

    token = iota((HALF, 1), 0)
    query_pos = jnp.concatenate(
        [((g << 5) + token).astype(f32) for g in groups for h in range(HEADS)], axis=0
    )
    contract = (((1,), (1,)), ((), ()))
    inside = (iota((1, 256), 1) & (HALF - 1)).astype(f32)
    pick_i = iota((16, 128), 1)
    picks = [onehot(pick_i == part) for part in range(2)]

    def scores(tile):
        q_a = q2[:, :, :, 128:].reshape(ROWS, LAT + 128)
        q_b = q2[:, :, :, 0 : LAT + 128].reshape(ROWS, LAT + 128)
        best = None
        for part, (q, k) in enumerate(
            ((q_a, kx[tile, :, 0 : LAT + 128]), (q_b, kx[tile, :, LAT:KEYS]))
        ):
            group = lax.dot_general(
                picks[part], kx[tile, :, KEYS:WIDE], contract, preferred_element_type=f32
            )[0:1, :]
            key_pos = group * float(HALF) + inside
            s = lax.dot_general(q, k, contract, preferred_element_type=f32)
            s = jnp.where(key_pos <= query_pos, s, masked_score)
            s_buf[tile, :, part * 256 : (part + 1) * 256] = s
            high = jnp.maximum(s[:, :128], s[:, 128:])
            best = high if best is None else jnp.maximum(best, high)
        if tile == 0:
            top[...] = best
        else:
            top[...] = jnp.maximum(top[...], best)

    def from_sibling(stage):
        for p in range(stage * 8, stage * 8 + 8):
            remote(
                slot_ref(p, 1), slot_ref(p, 1), sib_send.at[p], sib_recv.at[p], sibling
            ).wait_recv()

    scores(0)

    for k, (dx, dc) in enumerate(chip_peers):
        place = lax.rem(x + dx, NX) * 2 + lax.rem(core + dc, 2)
        remote(wp.at[place], wp.at[place], w1_send.at[0], w1_recv.at[place], sibling).wait_recv()
    own_weight.wait()
    to_i, from_i = iota((128, 128), 0), iota((128, 128), 1)
    regroup = onehot(
        from_i == (((to_i & 15) >> 1) << 4) + ((to_i >> 4) << 1) + (to_i & 1)
    )
    share = dot(regroup, wp[...].reshape(128, COLS)).astype(bf16).reshape(8, 16, COLS)

    def weight_slot(dz, half):
        nz = lax.rem(z + (dz + NZ), NZ)
        return wf.at[
            pl.ds(core * 8 + half * 4, 4), pl.ds(pl.multiple_of(nz * 16, 16), 16), :
        ]

    wf[pl.ds(core * 8, 8), pl.ds(pl.multiple_of(z * 16, 16), 16), :] = share
    ring_sends = []

    def weight_on(dz, half):
        index = (dz % NZ) * 2 + half
        here = weight_slot(dz, half)
        copy = remote(here, here, w3_send.at[index], w3_recv.at[index], sibling)
        copy.start()
        ring_sends.append(copy)
        steps = []
        if -3 < dz <= 0 or (dz == -3 and half == 0):
            steps.append(("z+", dz - 1))
        if 0 <= dz < 3 or (dz == 3 and half == 1):
            steps.append(("z-", dz + 1))
        for direction, there in steps:
            arrival = (there % NZ) * 2 + half
            copy = remote(
                here, here, w2_send.at[len(ring_sends) - 1], w2_recv.at[arrival], where[direction]
            )
            copy.start()
            ring_sends.append(copy)

    def weight_arrived(dz, half):
        index = (dz % NZ) * 2 + half
        here = weight_slot(dz, half)
        remote(here, here, w2_send.at[0], w2_recv.at[index], sibling).wait_recv()
        weight_on(dz, half)

    def weight_step(step):
        for half in range(2):
            if step < 4:
                weight_arrived(-step, half)
                weight_arrived(step, half)
            else:
                weight_arrived(-4 if half == 0 else 4, half)

    weight_on(0, 0)
    weight_on(0, 1)

    from_sibling(0)
    scores(1)
    for name in SLOTS[14:24]:
        arrived(name)
    scores(2)
    from_sibling(1)
    scores(3)
    for name in SLOTS[24:29]:
        arrived(name)
    scores(4)
    from_sibling(2)
    scores(5)
    weight_step(1)
    for name in SLOTS[29:32]:
        arrived(name)
    scores(6)
    from_sibling(3)
    scores(7)
    weight_step(2)

    load_av.wait()
    factor = SCALE * LOG2E
    chunk_rows = HALF * HEADS
    exchange = []
    for c in range(2):
        rows = slice(c * chunk_rows, (c + 1) * chunk_rows)
        peak = jnp.max(top[rows, :], axis=1, keepdims=True)
        total = jnp.zeros((chunk_rows, 128), f32)
        context = jnp.zeros((chunk_rows, LAT), f32)
        for tile in range(8):
            for part, cols in enumerate((slice(0, LAT), slice(LAT + 128, KEYS))):
                expo = jnp.exp2(
                    (s_buf[tile, rows, part * 256 : (part + 1) * 256] - peak) * factor
                )
                total = total + expo[:, :128] + expo[:, 128:]
                context = context + dot(expo.astype(bf16), kx[tile, :, cols])
        context = (context / jnp.sum(total, axis=1, keepdims=True)).astype(bf16)
        for h in range(HEADS):
            value = dot(context[h * HALF : (h + 1) * HALF], av[h])
            ho[c, x, :, h * VD : (h + 1) * VD] = value.astype(bf16)
        for k, direction in enumerate(("x+", "x-", "xx")):
            piece = ho.at[c, x]
            copy = remote(
                piece, piece, ho_send.at[c * 3 + k], ho_recv.at[c * 3 + k], where[direction]
            )
            copy.start()
            exchange.append(copy)
        weight_step(3 + c)
    for dz in range(NZ):
        for half in range(2):
            index = dz * 2 + half
            nz = lax.rem(z + dz, NZ)
            there = wf.at[
                pl.ds((1 - core) * 8 + half * 4, 4), pl.ds(pl.multiple_of(nz * 16, 16), 16), :
            ]
            remote(there, there, w3_send.at[0], w3_recv.at[index], sibling).wait_recv()

    def result_copy(c, nx):
        return remote(
            outs.at[c, nx], rcv.at[c, y], out_send.at[c * NX + nx], out_recv.at[c * NY + y],
            ((z * NX + nx) * 2 + core, x),
        )

    here = x == y
    for c in range(2):
        for k, dx in enumerate((3, 1, 2)):
            piece = ho.at[c, lax.rem(x + dx, NX)]
            remote(piece, piece, ho_send.at[0], ho_recv.at[c * 3 + k], sibling).wait_recv()
        product = dot(ho[c].reshape(NX * HALF, HEADS * VD), wf[...].reshape(HEADS * VD, COLS))
        outs[c] = product.astype(bf16).reshape(NX, HALF, COLS)
        for dx in (2, 1, 3, 0):
            nx = lax.rem(x + dx, NX)
            if dx == 0:

                @pl.when(here)
                def _():
                    pltpu.make_async_copy(
                        outs.at[c, nx], rcv.at[c, y], out_recv.at[c * NY + y]
                    ).start()

                @pl.when(jnp.logical_not(here))
                def _():
                    result_copy(c, nx).start()
            else:
                result_copy(c, nx).start()
    for c in range(2):
        final = jnp.zeros((HALF, COLS), f32)
        for k in range(NY):
            pltpu.make_async_copy(rcv.at[c, k], rcv.at[c, k], out_recv.at[c * NY + k]).wait()
            final = final + rcv[c, k].astype(f32)
        out_ref[c * HALF : (c + 1) * HALF, :] = final.astype(bf16)

    for c in range(2):
        for dx in range(NX):
            nx = lax.rem(x + dx, NX)
            if dx == 0:

                @pl.when(jnp.logical_not(here))
                def _():
                    result_copy(c, nx).wait_send()
            else:
                result_copy(c, nx).wait_send()
    for copy in pending + weight_sends + ring_sends + exchange:
        copy.wait_send()
    for k in range(len(SHARED_TO)):
        remote(slot_ref(0), slot_ref(0), key_send.at[60 + k], key_recv.at[0], sibling).wait_send()
    for p in range(32):
        remote(slot_ref(p), slot_ref(p), sib_send.at[p], sib_recv.at[p], sibling).wait_send()


def body(
    query_plain,
    query_rotary,
    latent_cache,
    key_rotary,
    latent_gain,
    positions,
    absorb_keys,
    absorb_values,
    output_weight,
):
    f32, bf16 = jnp.float32, jnp.bfloat16
    frequency = np.tile(rope_base ** (-np.arange(ROPE // 2) / (ROPE // 2)), 4)[None, :]
    inner = np.arange(HALF)[:, None] * frequency
    outer = np.arange(0, 4096, HALF)[:, None] * frequency
    tables = [f(a).astype(np.float32) for a in (outer, inner) for f in (np.cos, np.sin)]
    vmem = pl.BlockSpec(memory_space=pltpu.VMEM)
    hbm = pl.BlockSpec(memory_space=pl.ANY)
    dma = pltpu.SemaphoreType.DMA
    call = pl.pallas_call(
        kernel,
        out_shape=jax.ShapeDtypeStruct((TOK, COLS), bf16),
        in_specs=[pl.BlockSpec(memory_space=pltpu.SMEM)] + [vmem] * 9 + [hbm] * 2 + [vmem],
        out_specs=vmem,
        scratch_shapes=[
            pltpu.VMEM((HEADS, NOPE, LAT), bf16),
            pltpu.VMEM((HEADS, LAT, VD), bf16),
            pltpu.VMEM((8, 8 * HALF, WIDE), bf16),
            pltpu.VMEM((HEADS, TOK, NOPE), bf16),
            pltpu.VMEM((2, HEADS, HALF, LAT + 256), bf16),
            pltpu.VMEM((8, ROWS, 512), f32),
            pltpu.VMEM((ROWS, 128), f32),
            pltpu.VMEM((8, 16, COLS), bf16),
            pltpu.VMEM((HEADS, VD, COLS), bf16),
            pltpu.VMEM((2, NX, HALF, HEADS * VD), bf16),
            pltpu.VMEM((2, NX, HALF, COLS), bf16),
            pltpu.VMEM((2, NY, HALF, COLS), bf16),
            dma((3,)),
            dma((63,)),
            dma((32,)),
            dma((32,)),
            dma((32,)),
            dma((8,)),
            dma((8,)),
            dma((32,)),
            dma((16,)),
            dma((16,)),
            dma((16,)),
            dma((6,)),
            dma((6,)),
            dma((8,)),
            dma((8,)),
        ],
        compiler_params=pltpu.CompilerParams(
            collective_id=0, has_side_effects=True, vmem_limit_bytes=60 * 1024 * 1024
        ),
        cost_estimate=pl.CostEstimate(
            flops=11_000_000_000, bytes_accessed=6_000_000, transcendentals=4_200_000
        ),
    )
    return call(
        positions,
        query_plain.reshape(ROWS, NOPE),
        query_rotary.reshape(ROWS, ROPE),
        latent_cache,
        key_rotary,
        latent_gain.reshape(1, LAT),
        *tables,
        absorb_keys,
        absorb_values,
        output_weight.reshape(2 * HEADS, -1),
    )


def solution(mesh):
    return jax.shard_map(
        body,
        mesh=mesh,
        in_specs=(
            P("ctx", "head", None),
            P("ctx", "head", None),
            P("ctx", None),
            P("ctx", None),
            P(),
            P("ctx"),
            P("head", None, None),
            P("head", None, None),
            P("head", "ctx", None),
        ),
        out_specs=P("ctx", "head"),
        check_vma=False,
    )
```

```python
import jax
import jax.numpy as jnp
import numpy as np
from jax import lax
from jax.experimental import pallas as pl
from jax.experimental.pallas import tpu as pltpu
from jax.sharding import PartitionSpec as P

MESH = pl.DeviceIdType.MESH
norm_epsilon = 1e-06
rope_base = 10000.0
masked_score = -1e30

NZ, NX, NY = 8, 4, 4
TOK = 64
HALF = 32
PART = 16
CHUNKS = TOK // PART
HEADS = 16
ROWS = TOK * HEADS
NOPE, ROPE, LAT, VD = 128, 64, 512, 128
COLS = 896
KEYS = 2 * LAT + 2 * ROPE
WIDE = KEYS + 128
SCALE = 192 ** (-0.5)
LOG2E = 1.4426950408889634

SLOTS = [
    "own", "R1", "L1", "m0", "p0", "R2", "L2", "o0",
    "Ym", "Yp", "Yo", "R3", "L3", "R4", "mR3", "pR3",
    "Amm", "Apm", "Amp", "App", "Aom", "Aop", "Amo", "Apo",
    "Aoo", "oR3", "mL3", "pL3", "oL3", "mR4", "pR4", "oR4",
]
SLOT = {name: i for i, name in enumerate(SLOTS)}


def along_x(name):
    return [("x+", "m" + name), ("x-", "p" + name), ("xx", "o" + name)]


def along_y(name):
    return [("y+", "Am" + name), ("y-", "Ap" + name), ("yy", "Ao" + name)]


FORWARD = {
    "own": [("z+", "R1"), ("z-", "L1"), ("z++", "R2"), ("z--", "L2"), ("x+", "m0"), ("x-", "p0")],
    "m0": [("x+", "o0")],
    "R2": [("z+", "R3"), ("z++", "R4")],
    "L2": [("z-", "L3")],
    "R3": along_x("R3"),
    "L3": along_x("L3"),
    "R4": along_x("R4"),
    "Ym": along_y("m"),
    "Yp": along_y("p"),
    "Yo": along_y("o"),
}
SHARED = {"R1": 0, "L1": 1, "R2": 2, "L2": 3}
SHARED_TO = (("x+", "Ym"), ("x-", "Yp"), ("xx", "Yo"))


def kernel(
    pos_hbm, qp_hbm, qr_hbm, lat_hbm, kr_hbm, gain_hbm, cos_g_hbm, sin_g_hbm, cos_i_hbm, sin_i_hbm, ak_hbm, av_hbm,
    w_hbm,
    out_ref,
    pos_ref, qp_ref, qr_ref, lat_ref, kr_ref, gain_ref, cos_g, sin_g, cos_i, sin_i,
    ak, av, kx, qh, q2, s_buf, top, running_top, running_total, context_sum, wp, wf, ho, outs, rcv,
    local_sem, key_send, key_recv, sib_send, sib_recv, w1_send, w1_recv,
    w2_send, w2_recv, w3_send, w3_recv, ho_send, ho_recv, out_send, out_recv,
):
    f32, bf16 = jnp.float32, jnp.bfloat16
    me = lax.axis_index("ctx")
    y = lax.axis_index("head")
    core = lax.rem(me, 2)
    x = lax.rem(me // 2, NX)
    z = me // (2 * NX)

    def device(dz=0, dx=0, dc=0, dy=0):
        nz = lax.rem(z + (dz + NZ), NZ)
        nx = lax.rem(x + (dx + NX), NX)
        nc = lax.rem(core + dc, 2)
        ny = lax.rem(y + (dy + NY), NY)
        return ((nz * NX + nx) * 2 + nc, ny)

    sibling = device(dc=1)
    where = {
        "z+": device(dz=1), "z-": device(dz=-1), "x+": device(dx=1), "x-": device(dx=-1),
        "y+": device(dy=1), "y-": device(dy=-1),
        "z++": device(dz=2), "z--": device(dz=-2), "xx": device(dx=2), "yy": device(dy=2),
    }
    column_peers = [device(dz=d) for d in range(1, NZ)]
    chip_peers = [(dx, dc) for dx in range(NX) for dc in range(2) if (dx, dc) != (0, 0)]
    plane_peers = [device(dx=dx, dy=dy) for dx in range(NX) for dy in range(1, NY)]
    partners = column_peers + [device(dx=a, dc=b) for a, b in chip_peers] + plane_peers

    barrier = pltpu.get_barrier_semaphore()
    for partner in partners:
        pl.semaphore_signal(barrier, inc=1, device_id=partner, device_id_type=MESH)

    load_ak = pltpu.make_async_copy(ak_hbm, ak, local_sem.at[0])
    load_av = pltpu.make_async_copy(av_hbm, av, local_sem.at[1])
    loads = [
        pltpu.make_async_copy(source, target, local_sem.at[3 + k])
        for k, (source, target) in enumerate(
            (
                (pos_hbm, pos_ref), (lat_hbm, lat_ref), (kr_hbm, kr_ref), (gain_hbm, gain_ref),
                (cos_g_hbm, cos_g), (sin_g_hbm, sin_g), (cos_i_hbm, cos_i), (sin_i_hbm, sin_i),
                (qp_hbm, qp_ref), (qr_hbm, qr_ref),
            )
        )
    ]
    for load in loads:
        load.start()
    load_ak.start()
    load_av.start()

    def remote(src, dst, send, recv, to):
        return pltpu.make_async_remote_copy(
            src_ref=src, dst_ref=dst, send_sem=send, recv_sem=recv, device_id=to, device_id_type=MESH
        )

    def dot(a, b):
        return jnp.dot(a, b, preferred_element_type=f32)

    def iota(shape, axis):
        return lax.broadcasted_iota(jnp.int32, shape, axis)

    def onehot(mask):
        return jnp.where(mask, 1.0, 0.0).astype(bf16)

    def slot_ref(p, sib=0):
        return kx.at[2 * (p // 8) + sib, pl.ds((p % 8) * HALF, HALF), :]

    pending = []

    def send_block(p, to, dst):
        index = len(pending)
        copy = remote(slot_ref(p), slot_ref(dst), key_send.at[index], key_recv.at[dst], to)
        copy.start()
        pending.append(copy)

    def to_sibling(p):
        remote(slot_ref(p), slot_ref(p, 1), sib_send.at[p], sib_recv.at[p], sibling).start()

    def filled(name):
        p = SLOT[name]
        for direction, dst in FORWARD.get(name, []):
            send_block(p, where[direction], SLOT[dst])
        to_sibling(p)
        if name in SHARED:

            @pl.when(y == SHARED[name])
            def _():
                for k, (direction, dst) in enumerate(SHARED_TO):
                    remote(
                        slot_ref(p), slot_ref(SLOT[dst]), key_send.at[60 + k],
                        key_recv.at[SLOT[dst]], where[direction],
                    ).start()

    def arrived(name):
        p = SLOT[name]
        remote(slot_ref(p), slot_ref(p), key_send.at[0], key_recv.at[p], sibling).wait_recv()
        filled(name)

    for load in loads[:8]:
        load.wait()
    raw = lat_ref[...].astype(f32)
    spread = jnp.sum(raw * raw, axis=-1, keepdims=True) * (1.0 / LAT)
    latent = (raw * lax.rsqrt(spread + norm_epsilon) * gain_ref[...]).astype(bf16)
    row_i, col_i = iota((ROPE, 128), 0), iota((ROPE, 128), 1)
    low = iota((HALF, 128), 1) < ROPE
    kr = kr_ref[...]
    first = onehot(col_i == row_i)
    second = onehot(col_i == row_i + ROPE)
    turned = (row_i + HALF) & (ROPE - 1)
    first_turned = onehot(col_i == turned)
    second_turned = onehot(col_i == turned + ROPE)
    straight = dot(kr[:HALF], first) + dot(kr[HALF:], second)
    crossed = dot(kr[:HALF], first_turned) + dot(kr[HALF:], second_turned)
    groups = [pos_ref[0] >> 5, pos_ref[HALF] >> 5]
    cosines, sines = [], []
    for g in groups:
        c_g, s_g = cos_g[pl.ds(g, 1), :], sin_g[pl.ds(g, 1), :]
        cosines.append(c_g * cos_i[...] - s_g * sin_i[...])
        sines.append(s_g * cos_i[...] + c_g * sin_i[...])
    minus = jnp.where((iota((TOK, 128), 1) & (ROPE - 1)) < HALF, -1.0, 1.0)
    cosine = jnp.concatenate(cosines, axis=0)
    sine = jnp.concatenate(sines, axis=0) * minus
    key_rot = straight * jnp.where(low, cosine[:HALF], cosine[HALF:]) + crossed * jnp.where(
        low, sine[:HALF], sine[HALF:]
    )
    lane = iota((HALF, 128), 1)
    marks = jnp.where(
        lane == 0, groups[0].astype(f32), jnp.where(lane == 1, groups[1].astype(f32), 0.0)
    )
    kx[0, 0:HALF, 0:LAT] = latent[:HALF]
    kx[0, 0:HALF, LAT : LAT + 128] = key_rot.astype(bf16)
    kx[0, 0:HALF, LAT + 128 : KEYS] = latent[HALF:]
    kx[0, 0:HALF, KEYS:WIDE] = marks.astype(bf16)

    big_i, big_j = iota((256, 256), 0), iota((256, 256), 1)
    swap = onehot(big_j == ((big_i & 15) << 4) + (big_i >> 4))
    doubled = jnp.concatenate(
        [first + second, first_turned + second_turned], axis=1
    )
    low_q = iota((256, 128), 1) < ROPE
    for load in loads[8:]:
        load.wait()
    for b in range(TOK // 16):
        rows = slice(b * 256, (b + 1) * 256)
        plain = dot(swap, qp_ref[rows, :]).astype(bf16).reshape(HEADS, 16, NOPE)
        qh[:, b * 16 : (b + 1) * 16, :] = plain
        both = dot(swap, dot(qr_ref[rows, :], doubled).astype(bf16))
        tokens = slice(b * 16, (b + 1) * 16)
        c_rows = jnp.concatenate([cosine[tokens]] * HEADS, axis=0)
        s_rows = jnp.concatenate([sine[tokens]] * HEADS, axis=0)
        turned_q = both[:, :128] * c_rows + both[:, 128:] * s_rows
        q_first = jnp.where(low_q, turned_q, 0.0).astype(bf16).reshape(HEADS, 16, 128)
        q_second = jnp.where(low_q, 0.0, turned_q).astype(bf16).reshape(HEADS, 16, 128)
        q2[b, :, :, 0:128] = q_second
        q2[b, :, :, 128 + LAT :] = q_first
    load_ak.wait()
    for h in range(HEADS):
        absorbed = dot(qh[h], ak[h]).astype(bf16)
        for b in range(CHUNKS):
            q2[b, h, :, 128 : 128 + LAT] = absorbed[b * PART : (b + 1) * PART]

    pl.semaphore_wait(barrier, len(partners))

    filled("own")

    def weight_piece(nx, nc):
        return w_hbm.at[pl.ds(nc * 8, 8), :, pl.ds(pl.multiple_of(nx * COLS, 128), COLS)]

    my_place = x * 2 + core
    weight_sends = []
    for k, (dx, dc) in enumerate(chip_peers):
        nx, nc = lax.rem(x + dx, NX), lax.rem(core + dc, 2)
        copy = remote(
            weight_piece(nx, nc), wp.at[my_place], w1_send.at[k], w1_recv.at[my_place],
            device(dx=dx, dc=dc),
        )
        copy.start()
        weight_sends.append(copy)
    own_weight = pltpu.make_async_copy(weight_piece(x, core), wp.at[my_place], local_sem.at[2])
    own_weight.start()

    token = iota((PART, 1), 0)
    query_pos = [
        jnp.concatenate([((g << 5) + (token + start)).astype(f32)] * HEADS, axis=0)
        for g in groups
        for start in range(0, HALF, PART)
    ]
    contract = (((1,), (1,)), ((), ()))
    inside = (iota((1, 256), 1) & (HALF - 1)).astype(f32)
    pick_i = iota((16, 128), 1)
    picks = [onehot(pick_i == part) for part in range(2)]

    factor = SCALE * LOG2E
    chunk_rows = PART * HEADS

    def scores(tile, c):
        rows = slice(c * chunk_rows, (c + 1) * chunk_rows)
        q_a = q2[c, :, :, 128:].reshape(chunk_rows, LAT + 128)
        q_b = q2[c, :, :, 0 : LAT + 128].reshape(chunk_rows, LAT + 128)
        best = None
        for part, (q, k) in enumerate(
            ((q_a, kx[tile, :, 0 : LAT + 128]), (q_b, kx[tile, :, LAT:KEYS]))
        ):
            group = lax.dot_general(
                picks[part], kx[tile, :, KEYS:WIDE], contract, preferred_element_type=f32
            )[0:1, :]
            key_pos = group * float(HALF) + inside
            s = lax.dot_general(q, k, contract, preferred_element_type=f32)
            s = jnp.where(key_pos <= query_pos[c], s, masked_score)
            s_buf[tile % 2, rows, part * 256 : (part + 1) * 256] = s
            high = jnp.maximum(s[:, :128], s[:, 128:])
            best = high if best is None else jnp.maximum(best, high)
        top[tile % 2, rows, :] = best

    def update(stage, c):
        rows = slice(c * chunk_rows, (c + 1) * chunk_rows)
        peak = jnp.max(jnp.maximum(top[0, rows, :], top[1, rows, :]), axis=1, keepdims=True)
        if stage > 0:
            before = running_top[rows, 0:1]
            peak = jnp.maximum(before, peak)
            shrink = jnp.exp2((before - peak) * factor)
            total = running_total[rows, :] * shrink
        else:
            total = jnp.zeros((chunk_rows, 128), f32)
        grown = None
        for dc in range(2):
            tile = 2 * stage + dc
            for part, cols in enumerate((slice(0, LAT), slice(LAT + 128, KEYS))):
                expo = jnp.exp2((s_buf[dc, rows, part * 256 : (part + 1) * 256] - peak) * factor)
                total = total + expo[:, :128] + expo[:, 128:]
                product = dot(expo.astype(bf16), kx[tile, :, cols])
                grown = product if grown is None else grown + product
        if stage > 0:
            grown = grown + context_sum[rows, :] * shrink
        if stage < 3:
            running_top[rows, :] = jnp.broadcast_to(peak, (chunk_rows, 128))
            running_total[rows, :] = total
            context_sum[rows, :] = grown
        return grown, total

    def scores_all(tile):
        for c in range(CHUNKS):
            scores(tile, c)

    def update_all(stage):
        for c in range(CHUNKS):
            update(stage, c)

    def from_sibling(stage):
        for p in range(stage * 8, stage * 8 + 8):
            remote(
                slot_ref(p, 1), slot_ref(p, 1), sib_send.at[p], sib_recv.at[p], sibling
            ).wait_recv()

    def weight_slot(dz, half):
        nz = lax.rem(z + (dz + NZ), NZ)
        return wf.at[
            pl.ds(core * 8 + half * 4, 4), pl.ds(pl.multiple_of(nz * 16, 16), 16), :
        ]

    ring_sends = []

    def weight_on(dz, half):
        index = (dz % NZ) * 2 + half
        here = weight_slot(dz, half)
        copy = remote(here, here, w3_send.at[index], w3_recv.at[index], sibling)
        copy.start()
        ring_sends.append(copy)
        steps = []
        if -3 < dz <= 0 or (dz == -3 and half == 0):
            steps.append(("z+", dz - 1))
        if 0 <= dz < 3 or (dz == 3 and half == 1):
            steps.append(("z-", dz + 1))
        for direction, there in steps:
            arrival = (there % NZ) * 2 + half
            copy = remote(
                here, here, w2_send.at[len(ring_sends) - 1], w2_recv.at[arrival], where[direction]
            )
            copy.start()
            ring_sends.append(copy)

    def weight_arrived(dz, half):
        index = (dz % NZ) * 2 + half
        here = weight_slot(dz, half)
        remote(here, here, w2_send.at[0], w2_recv.at[index], sibling).wait_recv()
        weight_on(dz, half)

    def weight_step(step):
        for half in range(2):
            if step < 4:
                weight_arrived(-step, half)
                weight_arrived(step, half)
            else:
                weight_arrived(-4 if half == 0 else 4, half)

    def events(names):
        for name in names:
            arrived(name)

    events(SLOTS[1:8])
    scores_all(0)
    events(SLOTS[8:11])

    for k, (dx, dc) in enumerate(chip_peers):
        place = lax.rem(x + dx, NX) * 2 + lax.rem(core + dc, 2)
        remote(wp.at[place], wp.at[place], w1_send.at[0], w1_recv.at[place], sibling).wait_recv()
    own_weight.wait()
    to_i, from_i = iota((128, 128), 0), iota((128, 128), 1)
    regroup = onehot(
        from_i == (((to_i & 15) >> 1) << 4) + ((to_i >> 4) << 1) + (to_i & 1)
    )
    share = dot(regroup, wp[...].reshape(128, COLS)).astype(bf16).reshape(8, 16, COLS)

    wf[pl.ds(core * 8, 8), pl.ds(pl.multiple_of(z * 16, 16), 16), :] = share
    from_sibling(0)
    scores_all(1)
    events(SLOTS[11:13])
    weight_on(0, 0)
    weight_on(0, 1)
    update_all(0)
    events(SLOTS[13:16])
    weight_step(1)
    scores_all(2)
    events(SLOTS[16:24])
    from_sibling(1)
    scores_all(3)
    update_all(1)
    events(SLOTS[24:27])
    weight_step(2)
    scores_all(4)
    from_sibling(2)
    scores_all(5)
    update_all(2)
    events(SLOTS[27:32])
    scores_all(6)
    load_av.wait()
    from_sibling(3)

    exchange = []

    def head_out_copy(c, k, place, direction):
        piece = ho.at[c, place]
        if k >= 2:
            piece = ho.at[c, place, :, pl.ds((k - 2) * 1024, 1024)]
        return remote(
            piece, piece, ho_send.at[c * 4 + k], ho_recv.at[c * 4 + k], where[direction]
        )

    def head_out_send(*what):
        copy = head_out_copy(*what)
        copy.start()
        exchange.append(copy)

    from_left, from_right = lax.rem(x + 3, NX), lax.rem(x + 1, NX)
    opposite = lax.rem(x + 2, NX)
    for c in range(CHUNKS):
        scores(7, c)
        context, total = update(3, c)
        context = (context / jnp.sum(total, axis=1, keepdims=True)).astype(bf16)
        for h in range(HEADS):
            value = dot(context[h * PART : (h + 1) * PART], av[h])
            ho[c, x, :, h * VD : (h + 1) * VD] = value.astype(bf16)
        head_out_send(c, 0, x, "x+")
        head_out_send(c, 1, x, "x-")
    weight_step(3)
    for c in range(CHUNKS):
        head_out_copy(c, 0, from_left, "x+").wait_recv()
        head_out_send(c, 2, from_left, "x+")
        head_out_copy(c, 1, from_right, "x-").wait_recv()
        head_out_send(c, 3, from_right, "x-")
    weight_step(4)
    for dz in range(NZ):
        for half in range(2):
            index = dz * 2 + half
            nz = lax.rem(z + dz, NZ)
            there = wf.at[
                pl.ds((1 - core) * 8 + half * 4, 4), pl.ds(pl.multiple_of(nz * 16, 16), 16), :
            ]
            remote(there, there, w3_send.at[0], w3_recv.at[index], sibling).wait_recv()

    def result_copy(c, nx):
        return remote(
            outs.at[c, nx], rcv.at[c, y], out_send.at[c * NX + nx], out_recv.at[c * NY + y],
            ((z * NX + nx) * 2 + core, x),
        )

    here = x == y
    for c in range(CHUNKS):
        head_out_copy(c, 2, opposite, "x+").wait_recv()
        head_out_copy(c, 3, opposite, "x-").wait_recv()
        product = dot(ho[c].reshape(NX * PART, HEADS * VD), wf[...].reshape(HEADS * VD, COLS))
        outs[c] = product.astype(bf16).reshape(NX, PART, COLS)
        for dx in (2, 1, 3, 0):
            nx = lax.rem(x + dx, NX)
            if dx == 0:

                @pl.when(here)
                def _():
                    pltpu.make_async_copy(
                        outs.at[c, nx], rcv.at[c, y], out_recv.at[c * NY + y]
                    ).start()

                @pl.when(jnp.logical_not(here))
                def _():
                    result_copy(c, nx).start()
            else:
                result_copy(c, nx).start()
    for c in range(CHUNKS):
        final = jnp.zeros((PART, COLS), f32)
        for k in range(NY):
            pltpu.make_async_copy(rcv.at[c, k], rcv.at[c, k], out_recv.at[c * NY + k]).wait()
            final = final + rcv[c, k].astype(f32)
        out_ref[c * PART : (c + 1) * PART, :] = final.astype(bf16)

    for c in range(CHUNKS):
        for dx in range(NX):
            nx = lax.rem(x + dx, NX)
            if dx == 0:

                @pl.when(jnp.logical_not(here))
                def _():
                    result_copy(c, nx).wait_send()
            else:
                result_copy(c, nx).wait_send()
    for copy in pending + weight_sends + ring_sends + exchange:
        copy.wait_send()
    for k in range(len(SHARED_TO)):
        remote(slot_ref(0), slot_ref(0), key_send.at[60 + k], key_recv.at[0], sibling).wait_send()
    for p in range(32):
        remote(slot_ref(p), slot_ref(p), sib_send.at[p], sib_recv.at[p], sibling).wait_send()


def body(
    query_plain,
    query_rotary,
    latent_cache,
    key_rotary,
    latent_gain,
    positions,
    absorb_keys,
    absorb_values,
    output_weight,
):
    f32, bf16 = jnp.float32, jnp.bfloat16
    frequency = np.tile(rope_base ** (-np.arange(ROPE // 2) / (ROPE // 2)), 4)[None, :]
    inner = np.arange(HALF)[:, None] * frequency
    outer = np.arange(0, 4096, HALF)[:, None] * frequency
    tables = [f(a).astype(np.float32) for a in (outer, inner) for f in (np.cos, np.sin)]
    vmem = pl.BlockSpec(memory_space=pltpu.VMEM)
    hbm = pl.BlockSpec(memory_space=pl.ANY)
    dma = pltpu.SemaphoreType.DMA
    call = pl.pallas_call(
        kernel,
        out_shape=jax.ShapeDtypeStruct((TOK, COLS), bf16),
        in_specs=[hbm] * 13,
        out_specs=vmem,
        scratch_shapes=[
            pltpu.SMEM((TOK,), jnp.int32),
            pltpu.VMEM((ROWS, NOPE), bf16),
            pltpu.VMEM((ROWS, ROPE), bf16),
            pltpu.VMEM((TOK, LAT), bf16),
            pltpu.VMEM((TOK, ROPE), bf16),
            pltpu.VMEM((1, LAT), f32),
            pltpu.VMEM((128, 128), f32),
            pltpu.VMEM((128, 128), f32),
            pltpu.VMEM((HALF, 128), f32),
            pltpu.VMEM((HALF, 128), f32),
            pltpu.VMEM((HEADS, NOPE, LAT), bf16),
            pltpu.VMEM((HEADS, LAT, VD), bf16),
            pltpu.VMEM((8, 8 * HALF, WIDE), bf16),
            pltpu.VMEM((HEADS, TOK, NOPE), bf16),
            pltpu.VMEM((CHUNKS, HEADS, PART, LAT + 256), bf16),
            pltpu.VMEM((2, ROWS, 512), f32),
            pltpu.VMEM((2, ROWS, 128), f32),
            pltpu.VMEM((ROWS, 128), f32),
            pltpu.VMEM((ROWS, 128), f32),
            pltpu.VMEM((ROWS, LAT), f32),
            pltpu.VMEM((8, 8, 2, COLS), bf16),
            pltpu.VMEM((HEADS, VD, COLS), bf16),
            pltpu.VMEM((CHUNKS, NX, PART, HEADS * VD), bf16),
            pltpu.VMEM((CHUNKS, NX, PART, COLS), bf16),
            pltpu.VMEM((CHUNKS, NY, PART, COLS), bf16),
            dma((13,)),
            dma((63,)),
            dma((32,)),
            dma((32,)),
            dma((32,)),
            dma((8,)),
            dma((8,)),
            dma((32,)),
            dma((16,)),
            dma((16,)),
            dma((16,)),
            dma((4 * CHUNKS,)),
            dma((4 * CHUNKS,)),
            dma((NX * CHUNKS,)),
            dma((NY * CHUNKS,)),
        ],
        compiler_params=pltpu.CompilerParams(
            collective_id=0, has_side_effects=True, vmem_limit_bytes=60 * 1024 * 1024
        ),
        cost_estimate=pl.CostEstimate(
            flops=11_000_000_000, bytes_accessed=6_000_000, transcendentals=4_200_000
        ),
    )
    return call(
        positions,
        query_plain.reshape(ROWS, NOPE),
        query_rotary.reshape(ROWS, ROPE),
        latent_cache,
        key_rotary,
        latent_gain.reshape(1, LAT),
        *tables,
        absorb_keys,
        absorb_values,
        output_weight,
    )


def solution(mesh):
    return jax.shard_map(
        body,
        mesh=mesh,
        in_specs=(
            P("ctx", "head", None),
            P("ctx", "head", None),
            P("ctx", None),
            P("ctx", None),
            P(),
            P("ctx"),
            P("head", None, None),
            P("head", None, None),
            P("head", "ctx", None),
        ),
        out_specs=P("ctx", "head"),
        check_vma=False,
    )
```

```python
import jax
import jax.numpy as jnp
import numpy as np
from jax import lax
from jax.experimental import pallas as pl
from jax.experimental.pallas import tpu as pltpu
from jax.sharding import PartitionSpec as P

MESH = pl.DeviceIdType.MESH
norm_epsilon = 1e-06
rope_base = 10000.0
masked_score = -1e30

NZ, NX, NY = 8, 4, 4
TOK = 64
HALF = 32
PART = 16
CHUNKS = TOK // PART
HEADS = 16
ROWS = TOK * HEADS
NOPE, ROPE, LAT, VD = 128, 64, 512, 128
COLS = 896
KEYS = 2 * LAT + 2 * ROPE
WIDE = KEYS + 128
SCALE = 192 ** (-0.5)
LOG2E = 1.4426950408889634

SLOTS = [
    "own", "R1", "L1", "m0", "p0", "R2", "L2", "o0",
    "Ym", "Yp", "Yo", "R3", "L3", "R4", "mR3", "pR3",
    "Amm", "Apm", "Amp", "App", "Aom", "Aop", "Amo", "Apo",
    "Aoo", "oR3", "mL3", "pL3", "oL3", "mR4", "pR4", "oR4",
]
SLOT = {name: i for i, name in enumerate(SLOTS)}


def along_x(name):
    return [("x+", "m" + name), ("x-", "p" + name), ("xx", "o" + name)]


def along_y(name):
    return [("y+", "Am" + name), ("y-", "Ap" + name), ("yy", "Ao" + name)]


FORWARD = {
    "own": [("z+", "R1"), ("z-", "L1"), ("z++", "R2"), ("z--", "L2"), ("x+", "m0"), ("x-", "p0")],
    "m0": [("x+", "o0")],
    "R2": [("z+", "R3"), ("z++", "R4")],
    "L2": [("z-", "L3")],
    "R3": along_x("R3"),
    "L3": along_x("L3"),
    "R4": along_x("R4"),
    "Ym": along_y("m"),
    "Yp": along_y("p"),
    "Yo": along_y("o"),
}
SHARED = {"R1": 0, "L1": 1, "R2": 2, "L2": 3}
SHARED_TO = (("x+", "Ym"), ("x-", "Yp"), ("xx", "Yo"))


def kernel(
    pos_hbm, qp_hbm, qr_hbm, lat_hbm, kr_hbm, gain_hbm, cos_g_hbm, sin_g_hbm, cos_i_hbm, sin_i_hbm, ak_hbm, av_hbm,
    w_hbm,
    out_ref,
    pos_ref, qp_ref, qr_ref, lat_ref, kr_ref, gain_ref, cos_g, sin_g, cos_i, sin_i,
    ak, av, kx, qh, q2, s_buf, top, running_top, running_total, context_sum, wp, wf, ho, outs, rcv,
    local_sem, key_send, key_recv, sib_send, sib_recv, w1_send, w1_recv,
    w2_send, w2_recv, w3_send, w3_recv, ho_send, ho_recv, out_send, out_recv,
):
    f32, bf16 = jnp.float32, jnp.bfloat16
    me = lax.axis_index("ctx")
    y = lax.axis_index("head")
    core = lax.rem(me, 2)
    x = lax.rem(me // 2, NX)
    z = me // (2 * NX)

    def device(dz=0, dx=0, dc=0, dy=0):
        nz = lax.rem(z + (dz + NZ), NZ)
        nx = lax.rem(x + (dx + NX), NX)
        nc = lax.rem(core + dc, 2)
        ny = lax.rem(y + (dy + NY), NY)
        return ((nz * NX + nx) * 2 + nc, ny)

    sibling = device(dc=1)
    where = {
        "z+": device(dz=1), "z-": device(dz=-1), "x+": device(dx=1), "x-": device(dx=-1),
        "y+": device(dy=1), "y-": device(dy=-1),
        "z++": device(dz=2), "z--": device(dz=-2), "xx": device(dx=2), "yy": device(dy=2),
    }
    column_peers = [device(dz=d) for d in range(1, NZ)]
    chip_peers = [(dx, dc) for dx in range(NX) for dc in range(2) if (dx, dc) != (0, 0)]
    plane_peers = [device(dx=dx, dy=dy) for dx in range(NX) for dy in range(1, NY)]
    partners = column_peers + [device(dx=a, dc=b) for a, b in chip_peers] + plane_peers

    barrier = pltpu.get_barrier_semaphore()
    for partner in partners:
        pl.semaphore_signal(barrier, inc=1, device_id=partner, device_id_type=MESH)

    load_ak = pltpu.make_async_copy(ak_hbm, ak, local_sem.at[0])
    load_av = pltpu.make_async_copy(av_hbm, av, local_sem.at[1])
    loads = [
        pltpu.make_async_copy(source, target, local_sem.at[3 + k])
        for k, (source, target) in enumerate(
            (
                (pos_hbm, pos_ref), (lat_hbm, lat_ref), (kr_hbm, kr_ref), (gain_hbm, gain_ref),
                (cos_g_hbm, cos_g), (sin_g_hbm, sin_g), (cos_i_hbm, cos_i), (sin_i_hbm, sin_i),
                (qp_hbm, qp_ref), (qr_hbm, qr_ref),
            )
        )
    ]
    for load in loads:
        load.start()
    load_ak.start()
    load_av.start()

    def remote(src, dst, send, recv, to):
        return pltpu.make_async_remote_copy(
            src_ref=src, dst_ref=dst, send_sem=send, recv_sem=recv, device_id=to, device_id_type=MESH
        )

    def dot(a, b):
        return jnp.dot(a, b, preferred_element_type=f32)

    def iota(shape, axis):
        return lax.broadcasted_iota(jnp.int32, shape, axis)

    def onehot(mask):
        return jnp.where(mask, 1.0, 0.0).astype(bf16)

    def slot_ref(p, sib=0):
        return kx.at[2 * (p // 8) + sib, pl.ds((p % 8) * HALF, HALF), :]

    pending = []

    def send_block(p, to, dst):
        index = len(pending)
        copy = remote(slot_ref(p), slot_ref(dst), key_send.at[index], key_recv.at[dst], to)
        copy.start()
        pending.append(copy)

    def to_sibling(p):
        remote(slot_ref(p), slot_ref(p, 1), sib_send.at[p], sib_recv.at[p], sibling).start()

    def filled(name):
        p = SLOT[name]
        for direction, dst in FORWARD.get(name, []):
            send_block(p, where[direction], SLOT[dst])
        to_sibling(p)
        if name in SHARED:

            @pl.when(y == SHARED[name])
            def _():
                for k, (direction, dst) in enumerate(SHARED_TO):
                    remote(
                        slot_ref(p), slot_ref(SLOT[dst]), key_send.at[60 + k],
                        key_recv.at[SLOT[dst]], where[direction],
                    ).start()

    def arrived(name):
        p = SLOT[name]
        remote(slot_ref(p), slot_ref(p), key_send.at[0], key_recv.at[p], sibling).wait_recv()
        filled(name)

    for load in loads[:8]:
        load.wait()
    raw = lat_ref[...].astype(f32)
    spread = jnp.sum(raw * raw, axis=-1, keepdims=True) * (1.0 / LAT)
    latent = (raw * lax.rsqrt(spread + norm_epsilon) * gain_ref[...]).astype(bf16)
    row_i, col_i = iota((ROPE, 128), 0), iota((ROPE, 128), 1)
    low = iota((HALF, 128), 1) < ROPE
    kr = kr_ref[...]
    first = onehot(col_i == row_i)
    second = onehot(col_i == row_i + ROPE)
    turned = (row_i + HALF) & (ROPE - 1)
    first_turned = onehot(col_i == turned)
    second_turned = onehot(col_i == turned + ROPE)
    straight = dot(kr[:HALF], first) + dot(kr[HALF:], second)
    crossed = dot(kr[:HALF], first_turned) + dot(kr[HALF:], second_turned)
    groups = [pos_ref[0] >> 5, pos_ref[HALF] >> 5]
    cosines, sines = [], []
    for g in groups:
        c_g, s_g = cos_g[pl.ds(g, 1), :], sin_g[pl.ds(g, 1), :]
        cosines.append(c_g * cos_i[...] - s_g * sin_i[...])
        sines.append(s_g * cos_i[...] + c_g * sin_i[...])
    minus = jnp.where((iota((TOK, 128), 1) & (ROPE - 1)) < HALF, -1.0, 1.0)
    cosine = jnp.concatenate(cosines, axis=0)
    sine = jnp.concatenate(sines, axis=0) * minus
    key_rot = straight * jnp.where(low, cosine[:HALF], cosine[HALF:]) + crossed * jnp.where(
        low, sine[:HALF], sine[HALF:]
    )
    lane = iota((HALF, 128), 1)
    marks = jnp.where(
        lane == 0, groups[0].astype(f32), jnp.where(lane == 1, groups[1].astype(f32), 0.0)
    )
    kx[0, 0:HALF, 0:LAT] = latent[:HALF]
    kx[0, 0:HALF, LAT : LAT + 128] = key_rot.astype(bf16)
    kx[0, 0:HALF, LAT + 128 : KEYS] = latent[HALF:]
    kx[0, 0:HALF, KEYS:WIDE] = marks.astype(bf16)

    big_i, big_j = iota((256, 256), 0), iota((256, 256), 1)
    swap = onehot(big_j == ((big_i & 15) << 4) + (big_i >> 4))
    doubled = jnp.concatenate(
        [first + second, first_turned + second_turned], axis=1
    )
    low_q = iota((256, 128), 1) < ROPE
    for load in loads[8:]:
        load.wait()
    for b in range(TOK // 16):
        rows = slice(b * 256, (b + 1) * 256)
        plain = dot(swap, qp_ref[rows, :]).astype(bf16).reshape(HEADS, 16, NOPE)
        qh[:, b * 16 : (b + 1) * 16, :] = plain
        both = dot(swap, dot(qr_ref[rows, :], doubled).astype(bf16))
        tokens = slice(b * 16, (b + 1) * 16)
        c_rows = jnp.concatenate([cosine[tokens]] * HEADS, axis=0)
        s_rows = jnp.concatenate([sine[tokens]] * HEADS, axis=0)
        turned_q = both[:, :128] * c_rows + both[:, 128:] * s_rows
        q_first = jnp.where(low_q, turned_q, 0.0).astype(bf16).reshape(HEADS, 16, 128)
        q_second = jnp.where(low_q, 0.0, turned_q).astype(bf16).reshape(HEADS, 16, 128)
        q2[b, :, :, 0:128] = q_second
        q2[b, :, :, 128 + LAT :] = q_first
    load_ak.wait()
    for h in range(HEADS):
        absorbed = dot(qh[h], ak[h]).astype(bf16)
        for b in range(CHUNKS):
            q2[b, h, :, 128 : 128 + LAT] = absorbed[b * PART : (b + 1) * PART]

    pl.semaphore_wait(barrier, len(partners))

    filled("own")

    def weight_piece(nx, nc):
        return w_hbm.at[pl.ds(nc * 8, 8), :, pl.ds(pl.multiple_of(nx * COLS, 128), COLS)]

    my_place = x * 2 + core
    weight_sends = []
    for k, (dx, dc) in enumerate(chip_peers):
        nx, nc = lax.rem(x + dx, NX), lax.rem(core + dc, 2)
        copy = remote(
            weight_piece(nx, nc), wp.at[my_place], w1_send.at[k], w1_recv.at[my_place],
            device(dx=dx, dc=dc),
        )
        copy.start()
        weight_sends.append(copy)
    own_weight = pltpu.make_async_copy(weight_piece(x, core), wp.at[my_place], local_sem.at[2])
    own_weight.start()

    token = iota((PART, 1), 0)
    query_pos = [
        jnp.concatenate([((g << 5) + (token + start)).astype(f32)] * HEADS, axis=0)
        for g in groups
        for start in range(0, HALF, PART)
    ]
    contract = (((1,), (1,)), ((), ()))
    inside = (iota((1, 256), 1) & (HALF - 1)).astype(f32)
    pick_i = iota((16, 128), 1)
    picks = [onehot(pick_i == part) for part in range(2)]

    factor = SCALE * LOG2E
    chunk_rows = PART * HEADS

    def scores(tile, c):
        rows = slice(c * chunk_rows, (c + 1) * chunk_rows)
        q_a = q2[c, :, :, 128:].reshape(chunk_rows, LAT + 128)
        q_b = q2[c, :, :, 0 : LAT + 128].reshape(chunk_rows, LAT + 128)
        best = None
        for part, (q, k) in enumerate(
            ((q_a, kx[tile, :, 0 : LAT + 128]), (q_b, kx[tile, :, LAT:KEYS]))
        ):
            group = lax.dot_general(
                picks[part], kx[tile, :, KEYS:WIDE], contract, preferred_element_type=f32
            )[0:1, :]
            key_pos = group * float(HALF) + inside
            s = lax.dot_general(q, k, contract, preferred_element_type=f32)
            s = jnp.where(key_pos <= query_pos[c], s, masked_score)
            s_buf[tile % 2, rows, part * 256 : (part + 1) * 256] = s
            high = jnp.maximum(s[:, :128], s[:, 128:])
            best = high if best is None else jnp.maximum(best, high)
        top[tile % 2, rows, :] = best

    def update(stage, c):
        rows = slice(c * chunk_rows, (c + 1) * chunk_rows)
        peak = jnp.max(jnp.maximum(top[0, rows, :], top[1, rows, :]), axis=1, keepdims=True)
        if stage > 0:
            before = running_top[rows, 0:1]
            peak = jnp.maximum(before, peak)
            shrink = jnp.exp2((before - peak) * factor)
            total = running_total[rows, :] * shrink
        else:
            total = jnp.zeros((chunk_rows, 128), f32)
        grown = None
        for dc in range(2):
            tile = 2 * stage + dc
            for part, cols in enumerate((slice(0, LAT), slice(LAT + 128, KEYS))):
                expo = jnp.exp2((s_buf[dc, rows, part * 256 : (part + 1) * 256] - peak) * factor)
                total = total + expo[:, :128] + expo[:, 128:]
                product = dot(expo.astype(bf16), kx[tile, :, cols])
                grown = product if grown is None else grown + product
        if stage > 0:
            grown = grown + context_sum[rows, :] * shrink
        if stage < 3:
            running_top[rows, :] = jnp.broadcast_to(peak, (chunk_rows, 128))
            running_total[rows, :] = total
            context_sum[rows, :] = grown
        return grown, total

    def scores_all(tile):
        for c in range(CHUNKS):
            scores(tile, c)

    def update_all(stage):
        for c in range(CHUNKS):
            update(stage, c)

    def from_sibling(stage):
        for p in range(stage * 8, stage * 8 + 8):
            remote(
                slot_ref(p, 1), slot_ref(p, 1), sib_send.at[p], sib_recv.at[p], sibling
            ).wait_recv()

    def weight_slot(dz, half):
        nz = lax.rem(z + (dz + NZ), NZ)
        return wf.at[
            pl.ds(core * 8 + half * 4, 4), pl.ds(pl.multiple_of(nz * 16, 16), 16), :
        ]

    ring_sends = []

    def weight_on(dz, half):
        index = (dz % NZ) * 2 + half
        here = weight_slot(dz, half)
        copy = remote(here, here, w3_send.at[index], w3_recv.at[index], sibling)
        copy.start()
        ring_sends.append(copy)
        steps = []
        if -3 < dz <= 0:
            steps.append(("z+", dz - 1))
        if 0 <= dz < 3:
            steps.append(("z-", dz + 1))
        if dz == -2 and half == 0:
            steps.append(("z++", dz - 2))
        if dz == 2 and half == 1:
            steps.append(("z--", dz + 2))
        for direction, there in steps:
            arrival = (there % NZ) * 2 + half
            copy = remote(
                here, here, w2_send.at[len(ring_sends) - 1], w2_recv.at[arrival], where[direction]
            )
            copy.start()
            ring_sends.append(copy)

    def weight_arrived(dz, half):
        index = (dz % NZ) * 2 + half
        here = weight_slot(dz, half)
        remote(here, here, w2_send.at[0], w2_recv.at[index], sibling).wait_recv()
        weight_on(dz, half)

    def weight_step(step):
        for half in range(2):
            if step < 4:
                weight_arrived(-step, half)
                weight_arrived(step, half)
            else:
                weight_arrived(-4 if half == 0 else 4, half)

    def events(names):
        for name in names:
            arrived(name)

    events(SLOTS[1:8])
    scores_all(0)

    for k, (dx, dc) in enumerate(chip_peers):
        place = lax.rem(x + dx, NX) * 2 + lax.rem(core + dc, 2)
        remote(wp.at[place], wp.at[place], w1_send.at[0], w1_recv.at[place], sibling).wait_recv()
    own_weight.wait()
    to_i, from_i = iota((128, 128), 0), iota((128, 128), 1)
    regroup = onehot(
        from_i == (((to_i & 15) >> 1) << 4) + ((to_i >> 4) << 1) + (to_i & 1)
    )
    share = dot(regroup, wp[...].reshape(128, COLS)).astype(bf16).reshape(8, 16, COLS)

    wf[pl.ds(core * 8, 8), pl.ds(pl.multiple_of(z * 16, 16), 16), :] = share
    from_sibling(0)
    scores_all(1)
    events(["R3", "L3"])
    weight_on(0, 0)
    weight_on(0, 1)
    events(["Ym", "Yp", "Yo"])
    update_all(0)
    events(["R4", "mR3", "pR3"])
    scores_all(2)
    weight_step(1)
    events(SLOTS[16:20])
    from_sibling(1)
    scores_all(3)
    events(SLOTS[20:24])
    update_all(1)
    weight_step(2)
    scores_all(4)
    from_sibling(2)
    events(SLOTS[24:27])
    scores_all(5)
    events(SLOTS[27:29])
    update_all(2)
    events(SLOTS[29:32])
    scores_all(6)
    load_av.wait()
    from_sibling(3)

    exchange = []

    def head_out_copy(c, k, place, direction):
        piece = ho.at[c, place]
        if k >= 2:
            piece = ho.at[c, place, :, pl.ds((k - 2) * 1024, 1024)]
        return remote(
            piece, piece, ho_send.at[c * 4 + k], ho_recv.at[c * 4 + k], where[direction]
        )

    def head_out_send(*what):
        copy = head_out_copy(*what)
        copy.start()
        exchange.append(copy)

    from_left, from_right = lax.rem(x + 3, NX), lax.rem(x + 1, NX)
    opposite = lax.rem(x + 2, NX)
    for c in range(CHUNKS):
        scores(7, c)
        context, total = update(3, c)
        context = (context / jnp.sum(total, axis=1, keepdims=True)).astype(bf16)
        for h in range(HEADS):
            value = dot(context[h * PART : (h + 1) * PART], av[h])
            ho[c, x, :, h * VD : (h + 1) * VD] = value.astype(bf16)
        head_out_send(c, 0, x, "x+")
        head_out_send(c, 1, x, "x-")
    for c in range(CHUNKS):
        head_out_copy(c, 0, from_left, "x+").wait_recv()
        head_out_send(c, 2, from_left, "x+")
        head_out_copy(c, 1, from_right, "x-").wait_recv()
        head_out_send(c, 3, from_right, "x-")
    weight_step(3)
    weight_step(4)
    for dz in range(NZ):
        for half in range(2):
            index = dz * 2 + half
            nz = lax.rem(z + dz, NZ)
            there = wf.at[
                pl.ds((1 - core) * 8 + half * 4, 4), pl.ds(pl.multiple_of(nz * 16, 16), 16), :
            ]
            remote(there, there, w3_send.at[0], w3_recv.at[index], sibling).wait_recv()

    def result_copy(c, nx):
        return remote(
            outs.at[c, nx], rcv.at[c, y], out_send.at[c * NX + nx], out_recv.at[c * NY + y],
            ((z * NX + nx) * 2 + core, x),
        )

    here = x == y
    for c in range(CHUNKS):
        head_out_copy(c, 2, opposite, "x+").wait_recv()
        head_out_copy(c, 3, opposite, "x-").wait_recv()
        product = dot(ho[c].reshape(NX * PART, HEADS * VD), wf[...].reshape(HEADS * VD, COLS))
        outs[c] = product.astype(bf16).reshape(NX, PART, COLS)
        for dx in (2, 1, 3, 0):
            nx = lax.rem(x + dx, NX)
            if dx == 0:

                @pl.when(here)
                def _():
                    pltpu.make_async_copy(
                        outs.at[c, nx], rcv.at[c, y], out_recv.at[c * NY + y]
                    ).start()

                @pl.when(jnp.logical_not(here))
                def _():
                    result_copy(c, nx).start()
            else:
                result_copy(c, nx).start()
    for c in range(CHUNKS):
        final = jnp.zeros((PART, COLS), f32)
        for k in range(NY):
            pltpu.make_async_copy(rcv.at[c, k], rcv.at[c, k], out_recv.at[c * NY + k]).wait()
            final = final + rcv[c, k].astype(f32)
        out_ref[c * PART : (c + 1) * PART, :] = final.astype(bf16)

    for c in range(CHUNKS):
        for dx in range(NX):
            nx = lax.rem(x + dx, NX)
            if dx == 0:

                @pl.when(jnp.logical_not(here))
                def _():
                    result_copy(c, nx).wait_send()
            else:
                result_copy(c, nx).wait_send()
    for copy in pending + weight_sends + ring_sends + exchange:
        copy.wait_send()
    for k in range(len(SHARED_TO)):
        remote(slot_ref(0), slot_ref(0), key_send.at[60 + k], key_recv.at[0], sibling).wait_send()
    for p in range(32):
        remote(slot_ref(p), slot_ref(p), sib_send.at[p], sib_recv.at[p], sibling).wait_send()


def body(
    query_plain,
    query_rotary,
    latent_cache,
    key_rotary,
    latent_gain,
    positions,
    absorb_keys,
    absorb_values,
    output_weight,
):
    f32, bf16 = jnp.float32, jnp.bfloat16
    frequency = np.tile(rope_base ** (-np.arange(ROPE // 2) / (ROPE // 2)), 4)[None, :]
    inner = np.arange(HALF)[:, None] * frequency
    outer = np.arange(0, 4096, HALF)[:, None] * frequency
    tables = [f(a).astype(np.float32) for a in (outer, inner) for f in (np.cos, np.sin)]
    vmem = pl.BlockSpec(memory_space=pltpu.VMEM)
    hbm = pl.BlockSpec(memory_space=pl.ANY)
    dma = pltpu.SemaphoreType.DMA
    call = pl.pallas_call(
        kernel,
        out_shape=jax.ShapeDtypeStruct((TOK, COLS), bf16),
        in_specs=[hbm] * 13,
        out_specs=vmem,
        scratch_shapes=[
            pltpu.SMEM((TOK,), jnp.int32),
            pltpu.VMEM((ROWS, NOPE), bf16),
            pltpu.VMEM((ROWS, ROPE), bf16),
            pltpu.VMEM((TOK, LAT), bf16),
            pltpu.VMEM((TOK, ROPE), bf16),
            pltpu.VMEM((1, LAT), f32),
            pltpu.VMEM((128, 128), f32),
            pltpu.VMEM((128, 128), f32),
            pltpu.VMEM((HALF, 128), f32),
            pltpu.VMEM((HALF, 128), f32),
            pltpu.VMEM((HEADS, NOPE, LAT), bf16),
            pltpu.VMEM((HEADS, LAT, VD), bf16),
            pltpu.VMEM((8, 8 * HALF, WIDE), bf16),
            pltpu.VMEM((HEADS, TOK, NOPE), bf16),
            pltpu.VMEM((CHUNKS, HEADS, PART, LAT + 256), bf16),
            pltpu.VMEM((2, ROWS, 512), f32),
            pltpu.VMEM((2, ROWS, 128), f32),
            pltpu.VMEM((ROWS, 128), f32),
            pltpu.VMEM((ROWS, 128), f32),
            pltpu.VMEM((ROWS, LAT), f32),
            pltpu.VMEM((8, 8, 2, COLS), bf16),
            pltpu.VMEM((HEADS, VD, COLS), bf16),
            pltpu.VMEM((CHUNKS, NX, PART, HEADS * VD), bf16),
            pltpu.VMEM((CHUNKS, NX, PART, COLS), bf16),
            pltpu.VMEM((CHUNKS, NY, PART, COLS), bf16),
            dma((13,)),
            dma((63,)),
            dma((32,)),
            dma((32,)),
            dma((32,)),
            dma((8,)),
            dma((8,)),
            dma((32,)),
            dma((16,)),
            dma((16,)),
            dma((16,)),
            dma((4 * CHUNKS,)),
            dma((4 * CHUNKS,)),
            dma((NX * CHUNKS,)),
            dma((NY * CHUNKS,)),
        ],
        compiler_params=pltpu.CompilerParams(
            collective_id=0, has_side_effects=True, vmem_limit_bytes=60 * 1024 * 1024
        ),
        cost_estimate=pl.CostEstimate(
            flops=11_000_000_000, bytes_accessed=6_000_000, transcendentals=4_200_000
        ),
    )
    return call(
        positions,
        query_plain.reshape(ROWS, NOPE),
        query_rotary.reshape(ROWS, ROPE),
        latent_cache,
        key_rotary,
        latent_gain.reshape(1, LAT),
        *tables,
        absorb_keys,
        absorb_values,
        output_weight,
    )


def solution(mesh):
    return jax.shard_map(
        body,
        mesh=mesh,
        in_specs=(
            P("ctx", "head", None),
            P("ctx", "head", None),
            P("ctx", None),
            P("ctx", None),
            P(),
            P("ctx"),
            P("head", None, None),
            P("head", None, None),
            P("head", "ctx", None),
        ),
        out_specs=P("ctx", "head"),
        check_vma=False,
    )
```

```python
import jax
import jax.numpy as jnp
import numpy as np
from jax import lax
from jax.experimental import pallas as pl
from jax.experimental.pallas import tpu as pltpu
from jax.sharding import PartitionSpec as P

MESH = pl.DeviceIdType.MESH
norm_epsilon = 1e-06
rope_base = 10000.0
masked_score = -1e30

NZ, NX, NY = 8, 4, 4
TOK = 64
HALF = 32
PART = 16
CHUNKS = TOK // PART
HEADS = 16
ROWS = TOK * HEADS
NOPE, ROPE, LAT, VD = 128, 64, 512, 128
COLS = 896
KEYS = 2 * LAT + 2 * ROPE
WIDE = KEYS + 128
SCALE = 192 ** (-0.5)
LOG2E = 1.4426950408889634

SLOTS = [
    "own", "R1", "L1", "m0", "p0", "R2", "L2", "o0",
    "Ym", "Yp", "Yo", "R3", "L3", "R4", "mR3", "pR3",
    "Amm", "Apm", "Amp", "App", "Aom", "Aop", "Amo", "Apo",
    "Aoo", "oR3", "mL3", "pL3", "oL3", "mR4", "pR4", "oR4",
]
SLOT = {name: i for i, name in enumerate(SLOTS)}


def along_x(name):
    return [("x+", "m" + name), ("x-", "p" + name), ("xx", "o" + name)]


def along_y(name):
    return [("y+", "Am" + name), ("y-", "Ap" + name), ("yy", "Ao" + name)]


FORWARD = {
    "own": [("z+", "R1"), ("z-", "L1"), ("z++", "R2"), ("z--", "L2"), ("x+", "m0"), ("x-", "p0")],
    "m0": [("x+", "o0")],
    "R2": [("z+", "R3"), ("z++", "R4")],
    "L2": [("z-", "L3")],
    "R3": along_x("R3"),
    "L3": along_x("L3"),
    "R4": along_x("R4"),
    "Ym": along_y("m"),
    "Yp": along_y("p"),
    "Yo": along_y("o"),
}
SHARED = {"R1": 0, "L1": 1, "R2": 2, "L2": 3}
SHARED_TO = (("x+", "Ym"), ("x-", "Yp"), ("xx", "Yo"))


def kernel(
    pos_hbm, qp_hbm, qr_hbm, lat_hbm, kr_hbm, gain_hbm, cos_g_hbm, sin_g_hbm, cos_i_hbm, sin_i_hbm, ak_hbm, av_hbm,
    w_hbm,
    out_ref,
    pos_ref, qp_ref, qr_ref, lat_ref, kr_ref, gain_ref, cos_g, sin_g, cos_i, sin_i,
    ak, av, kx, qh, q2, s_buf, top, running_top, running_total, context_sum, wp, wf, ho, outs, rcv,
    local_sem, key_send, key_recv, sib_send, sib_recv, w1_send, w1_recv,
    w2_send, w2_recv, w3_send, w3_recv, ho_send, ho_recv, out_send, out_recv,
):
    f32, bf16 = jnp.float32, jnp.bfloat16
    me = lax.axis_index("ctx")
    y = lax.axis_index("head")
    core = lax.rem(me, 2)
    x = lax.rem(me // 2, NX)
    z = me // (2 * NX)

    def device(dz=0, dx=0, dc=0, dy=0):
        nz = lax.rem(z + (dz + NZ), NZ)
        nx = lax.rem(x + (dx + NX), NX)
        nc = lax.rem(core + dc, 2)
        ny = lax.rem(y + (dy + NY), NY)
        return ((nz * NX + nx) * 2 + nc, ny)

    sibling = device(dc=1)
    where = {
        "z+": device(dz=1), "z-": device(dz=-1), "x+": device(dx=1), "x-": device(dx=-1),
        "y+": device(dy=1), "y-": device(dy=-1),
        "z++": device(dz=2), "z--": device(dz=-2), "xx": device(dx=2), "yy": device(dy=2),
    }
    column_peers = [device(dz=d) for d in range(1, NZ)]
    chip_peers = [(dx, dc) for dx in range(NX) for dc in range(2) if (dx, dc) != (0, 0)]
    plane_peers = [device(dx=dx, dy=dy) for dx in range(NX) for dy in range(1, NY)]
    partners = column_peers + [device(dx=a, dc=b) for a, b in chip_peers] + plane_peers

    barrier = pltpu.get_barrier_semaphore()
    for partner in partners:
        pl.semaphore_signal(barrier, inc=1, device_id=partner, device_id_type=MESH)

    load_ak = pltpu.make_async_copy(ak_hbm, ak, local_sem.at[0])
    load_av = pltpu.make_async_copy(av_hbm, av, local_sem.at[1])
    loads = [
        pltpu.make_async_copy(source, target, local_sem.at[3 + k])
        for k, (source, target) in enumerate(
            (
                (pos_hbm, pos_ref), (lat_hbm, lat_ref), (kr_hbm, kr_ref), (gain_hbm, gain_ref),
                (cos_g_hbm, cos_g), (sin_g_hbm, sin_g), (cos_i_hbm, cos_i), (sin_i_hbm, sin_i),
                (qp_hbm, qp_ref), (qr_hbm, qr_ref),
            )
        )
    ]
    for load in loads:
        load.start()
    load_ak.start()
    load_av.start()

    def remote(src, dst, send, recv, to):
        return pltpu.make_async_remote_copy(
            src_ref=src, dst_ref=dst, send_sem=send, recv_sem=recv, device_id=to, device_id_type=MESH
        )

    def dot(a, b):
        return jnp.dot(a, b, preferred_element_type=f32)

    def iota(shape, axis):
        return lax.broadcasted_iota(jnp.int32, shape, axis)

    def onehot(mask):
        return jnp.where(mask, 1.0, 0.0).astype(bf16)

    def slot_ref(p, sib=0):
        return kx.at[2 * (p // 8) + sib, pl.ds((p % 8) * HALF, HALF), :]

    pending = []

    def send_block(p, to, dst):
        index = len(pending)
        copy = remote(slot_ref(p), slot_ref(dst), key_send.at[index], key_recv.at[dst], to)
        copy.start()
        pending.append(copy)

    def to_sibling(p):
        remote(slot_ref(p), slot_ref(p, 1), sib_send.at[p], sib_recv.at[p], sibling).start()

    def filled(name):
        p = SLOT[name]
        for direction, dst in FORWARD.get(name, []):
            send_block(p, where[direction], SLOT[dst])
        to_sibling(p)
        if name in SHARED:

            @pl.when(y == SHARED[name])
            def _():
                for k, (direction, dst) in enumerate(SHARED_TO):
                    remote(
                        slot_ref(p), slot_ref(SLOT[dst]), key_send.at[60 + k],
                        key_recv.at[SLOT[dst]], where[direction],
                    ).start()

    def arrived(name):
        p = SLOT[name]
        remote(slot_ref(p), slot_ref(p), key_send.at[0], key_recv.at[p], sibling).wait_recv()
        filled(name)

    for load in loads[:8]:
        load.wait()
    raw = lat_ref[...].astype(f32)
    spread = jnp.sum(raw * raw, axis=-1, keepdims=True) * (1.0 / LAT)
    latent = (raw * lax.rsqrt(spread + norm_epsilon) * gain_ref[...]).astype(bf16)
    row_i, col_i = iota((ROPE, 128), 0), iota((ROPE, 128), 1)
    low = iota((HALF, 128), 1) < ROPE
    kr = kr_ref[...]
    first = onehot(col_i == row_i)
    second = onehot(col_i == row_i + ROPE)
    turned = (row_i + HALF) & (ROPE - 1)
    first_turned = onehot(col_i == turned)
    second_turned = onehot(col_i == turned + ROPE)
    straight = dot(kr[:HALF], first) + dot(kr[HALF:], second)
    crossed = dot(kr[:HALF], first_turned) + dot(kr[HALF:], second_turned)
    groups = [pos_ref[0] >> 5, pos_ref[HALF] >> 5]
    cosines, sines = [], []
    for g in groups:
        c_g, s_g = cos_g[pl.ds(g, 1), :], sin_g[pl.ds(g, 1), :]
        cosines.append(c_g * cos_i[...] - s_g * sin_i[...])
        sines.append(s_g * cos_i[...] + c_g * sin_i[...])
    minus = jnp.where((iota((TOK, 128), 1) & (ROPE - 1)) < HALF, -1.0, 1.0)
    cosine = jnp.concatenate(cosines, axis=0)
    sine = jnp.concatenate(sines, axis=0) * minus
    key_rot = straight * jnp.where(low, cosine[:HALF], cosine[HALF:]) + crossed * jnp.where(
        low, sine[:HALF], sine[HALF:]
    )
    lane = iota((HALF, 128), 1)
    marks = jnp.where(
        lane == 0, groups[0].astype(f32), jnp.where(lane == 1, groups[1].astype(f32), 0.0)
    )
    kx[0, 0:HALF, 0:LAT] = latent[:HALF]
    kx[0, 0:HALF, LAT : LAT + 128] = key_rot.astype(bf16)
    kx[0, 0:HALF, LAT + 128 : KEYS] = latent[HALF:]
    kx[0, 0:HALF, KEYS:WIDE] = marks.astype(bf16)

    big_i, big_j = iota((256, 256), 0), iota((256, 256), 1)
    swap = onehot(big_j == ((big_i & 15) << 4) + (big_i >> 4))
    doubled = jnp.concatenate(
        [first + second, first_turned + second_turned], axis=1
    )
    low_q = iota((256, 128), 1) < ROPE
    for load in loads[8:]:
        load.wait()
    for b in range(TOK // 16):
        rows = slice(b * 256, (b + 1) * 256)
        plain = dot(swap, qp_ref[rows, :]).astype(bf16).reshape(HEADS, 16, NOPE)
        qh[:, b * 16 : (b + 1) * 16, :] = plain
        both = dot(swap, dot(qr_ref[rows, :], doubled).astype(bf16))
        tokens = slice(b * 16, (b + 1) * 16)
        c_rows = jnp.concatenate([cosine[tokens]] * HEADS, axis=0)
        s_rows = jnp.concatenate([sine[tokens]] * HEADS, axis=0)
        turned_q = both[:, :128] * c_rows + both[:, 128:] * s_rows
        q_first = jnp.where(low_q, turned_q, 0.0).astype(bf16).reshape(HEADS, 16, 128)
        q_second = jnp.where(low_q, 0.0, turned_q).astype(bf16).reshape(HEADS, 16, 128)
        q2[b, :, :, 0:128] = q_second
        q2[b, :, :, 128 + LAT :] = q_first
    load_ak.wait()
    for h in range(HEADS):
        absorbed = dot(qh[h], ak[h]).astype(bf16)
        for b in range(CHUNKS):
            q2[b, h, :, 128 : 128 + LAT] = absorbed[b * PART : (b + 1) * PART]

    pl.semaphore_wait(barrier, len(partners))

    filled("own")

    def weight_piece(nx, nc):
        return w_hbm.at[pl.ds(nc * 8, 8), :, pl.ds(pl.multiple_of(nx * COLS, 128), COLS)]

    my_place = x * 2 + core
    weight_sends = []
    for k, (dx, dc) in enumerate(chip_peers):
        nx, nc = lax.rem(x + dx, NX), lax.rem(core + dc, 2)
        copy = remote(
            weight_piece(nx, nc), wp.at[my_place], w1_send.at[k], w1_recv.at[my_place],
            device(dx=dx, dc=dc),
        )
        copy.start()
        weight_sends.append(copy)
    own_weight = pltpu.make_async_copy(weight_piece(x, core), wp.at[my_place], local_sem.at[2])
    own_weight.start()

    token = iota((PART, 1), 0)
    query_pos = [
        jnp.concatenate([((g << 5) + (token + start)).astype(f32)] * HEADS, axis=0)
        for g in groups
        for start in range(0, HALF, PART)
    ]
    contract = (((1,), (1,)), ((), ()))
    inside = (iota((1, 256), 1) & (HALF - 1)).astype(f32)
    pick_i = iota((16, 128), 1)
    picks = [onehot(pick_i == part) for part in range(2)]

    factor = SCALE * LOG2E
    chunk_rows = PART * HEADS

    def scores(tile, c):
        rows = slice(c * chunk_rows, (c + 1) * chunk_rows)
        q_a = q2[c, :, :, 128:].reshape(chunk_rows, LAT + 128)
        q_b = q2[c, :, :, 0 : LAT + 128].reshape(chunk_rows, LAT + 128)
        best = None
        for part, (q, k) in enumerate(
            ((q_a, kx[tile, :, 0 : LAT + 128]), (q_b, kx[tile, :, LAT:KEYS]))
        ):
            group = lax.dot_general(
                picks[part], kx[tile, :, KEYS:WIDE], contract, preferred_element_type=f32
            )[0:1, :]
            key_pos = group * float(HALF) + inside
            s = lax.dot_general(q, k, contract, preferred_element_type=f32)
            s = jnp.where(key_pos <= query_pos[c], s, masked_score)
            s_buf[tile % 2, rows, part * 256 : (part + 1) * 256] = s
            high = jnp.maximum(s[:, :128], s[:, 128:])
            best = high if best is None else jnp.maximum(best, high)
        top[tile % 2, rows, :] = best

    def update(stage, c):
        rows = slice(c * chunk_rows, (c + 1) * chunk_rows)
        peak = jnp.max(jnp.maximum(top[0, rows, :], top[1, rows, :]), axis=1, keepdims=True)
        if stage > 0:
            before = running_top[rows, 0:1]
            peak = jnp.maximum(before, peak)
            shrink = jnp.exp2((before - peak) * factor)
            total = running_total[rows, :] * shrink
        else:
            total = jnp.zeros((chunk_rows, 128), f32)
        grown = None
        for dc in range(2):
            tile = 2 * stage + dc
            for part, cols in enumerate((slice(0, LAT), slice(LAT + 128, KEYS))):
                expo = jnp.exp2((s_buf[dc, rows, part * 256 : (part + 1) * 256] - peak) * factor)
                total = total + expo[:, :128] + expo[:, 128:]
                product = dot(expo.astype(bf16), kx[tile, :, cols])
                grown = product if grown is None else grown + product
        if stage > 0:
            grown = grown + context_sum[rows, :] * shrink
        if stage < 3:
            running_top[rows, :] = jnp.broadcast_to(peak, (chunk_rows, 128))
            running_total[rows, :] = total
            context_sum[rows, :] = grown
        return grown, total

    def scores_all(tile):
        for c in range(CHUNKS):
            scores(tile, c)

    def update_all(stage):
        for c in range(CHUNKS):
            update(stage, c)

    def from_sibling(stage):
        for p in range(stage * 8, stage * 8 + 8):
            remote(
                slot_ref(p, 1), slot_ref(p, 1), sib_send.at[p], sib_recv.at[p], sibling
            ).wait_recv()

    def weight_slot(dz, half):
        nz = lax.rem(z + (dz + NZ), NZ)
        return wf.at[
            pl.ds(core * 8 + half * 4, 4), pl.ds(pl.multiple_of(nz * 16, 16), 16), :
        ]

    ring_sends = []

    def weight_on(dz, half):
        index = (dz % NZ) * 2 + half
        here = weight_slot(dz, half)
        copy = remote(here, here, w3_send.at[index], w3_recv.at[index], sibling)
        copy.start()
        ring_sends.append(copy)
        steps = []
        if -3 < dz <= 0:
            steps.append(("z+", dz - 1))
        if 0 <= dz < 3:
            steps.append(("z-", dz + 1))
        if dz == -2 and half == 0:
            steps.append(("z++", dz - 2))
        if dz == 2 and half == 1:
            steps.append(("z--", dz + 2))
        for direction, there in steps:
            arrival = (there % NZ) * 2 + half
            copy = remote(
                here, here, w2_send.at[len(ring_sends) - 1], w2_recv.at[arrival], where[direction]
            )
            copy.start()
            ring_sends.append(copy)

    def weight_arrived(dz, half):
        index = (dz % NZ) * 2 + half
        here = weight_slot(dz, half)
        remote(here, here, w2_send.at[0], w2_recv.at[index], sibling).wait_recv()
        weight_on(dz, half)

    def weight_step(step):
        for half in range(2):
            if step < 4:
                weight_arrived(-step, half)
                weight_arrived(step, half)
            else:
                weight_arrived(-4 if half == 0 else 4, half)

    def events(names):
        for name in names:
            arrived(name)

    events(SLOTS[1:8])
    scores_all(0)

    for k, (dx, dc) in enumerate(chip_peers):
        place = lax.rem(x + dx, NX) * 2 + lax.rem(core + dc, 2)
        remote(wp.at[place], wp.at[place], w1_send.at[0], w1_recv.at[place], sibling).wait_recv()
    own_weight.wait()
    to_i, from_i = iota((128, 128), 0), iota((128, 128), 1)
    regroup = onehot(
        from_i == (((to_i & 15) >> 1) << 4) + ((to_i >> 4) << 1) + (to_i & 1)
    )
    share = dot(regroup, wp[...].reshape(128, COLS)).astype(bf16).reshape(8, 16, COLS)

    wf[pl.ds(core * 8, 8), pl.ds(pl.multiple_of(z * 16, 16), 16), :] = share
    from_sibling(0)
    scores_all(1)
    events(["R3", "L3"])
    weight_on(0, 0)
    weight_on(0, 1)
    events(["Ym", "Yp", "Yo"])
    update_all(0)
    events(["R4", "mR3", "pR3"])
    scores_all(2)
    weight_step(1)
    events(SLOTS[16:20])
    from_sibling(1)
    scores_all(3)
    events(SLOTS[20:24])
    update_all(1)
    weight_step(2)
    scores_all(4)
    from_sibling(2)
    events(SLOTS[24:27])
    scores_all(5)
    events(SLOTS[27:29])
    update_all(2)
    events(SLOTS[29:32])
    scores_all(6)
    load_av.wait()
    from_sibling(3)

    exchange = []

    def head_out_copy(c, k, place, direction):
        piece = ho.at[c, place]
        if k >= 2:
            piece = ho.at[c, place, :, pl.ds((k - 2) * 1024, 1024)]
        return remote(
            piece, piece, ho_send.at[c * 4 + k], ho_recv.at[c * 4 + k], where[direction]
        )

    def head_out_send(*what):
        copy = head_out_copy(*what)
        copy.start()
        exchange.append(copy)

    from_left, from_right = lax.rem(x + 3, NX), lax.rem(x + 1, NX)
    opposite = lax.rem(x + 2, NX)
    for c in range(CHUNKS):
        scores(7, c)
        context, total = update(3, c)
        context = (context / jnp.sum(total, axis=1, keepdims=True)).astype(bf16)
        for h in range(HEADS):
            value = dot(context[h * PART : (h + 1) * PART], av[h])
            ho[c, x, :, h * VD : (h + 1) * VD] = value.astype(bf16)
        head_out_send(c, 0, x, "x+")
        head_out_send(c, 1, x, "x-")
    weight_step(3)
    for c in range(CHUNKS):
        if c == 2:
            weight_step(4)
        head_out_copy(c, 0, from_left, "x+").wait_recv()
        head_out_send(c, 2, from_left, "x+")
        head_out_copy(c, 1, from_right, "x-").wait_recv()
        head_out_send(c, 3, from_right, "x-")
    for dz in range(NZ):
        for half in range(2):
            index = dz * 2 + half
            nz = lax.rem(z + dz, NZ)
            there = wf.at[
                pl.ds((1 - core) * 8 + half * 4, 4), pl.ds(pl.multiple_of(nz * 16, 16), 16), :
            ]
            remote(there, there, w3_send.at[0], w3_recv.at[index], sibling).wait_recv()

    def result_copy(c, nx):
        return remote(
            outs.at[c, nx], rcv.at[c, y], out_send.at[c * NX + nx], out_recv.at[c * NY + y],
            ((z * NX + nx) * 2 + core, x),
        )

    here = x == y
    for c in range(CHUNKS):
        head_out_copy(c, 2, opposite, "x+").wait_recv()
        head_out_copy(c, 3, opposite, "x-").wait_recv()
        product = dot(ho[c].reshape(NX * PART, HEADS * VD), wf[...].reshape(HEADS * VD, COLS))
        outs[c] = product.astype(bf16).reshape(NX, PART, COLS)
        for dx in (2, 1, 3, 0):
            nx = lax.rem(x + dx, NX)
            if dx == 0:

                @pl.when(here)
                def _():
                    pltpu.make_async_copy(
                        outs.at[c, nx], rcv.at[c, y], out_recv.at[c * NY + y]
                    ).start()

                @pl.when(jnp.logical_not(here))
                def _():
                    result_copy(c, nx).start()
            else:
                result_copy(c, nx).start()
    for c in range(CHUNKS):
        final = jnp.zeros((PART, COLS), f32)
        for k in range(NY):
            pltpu.make_async_copy(rcv.at[c, k], rcv.at[c, k], out_recv.at[c * NY + k]).wait()
            final = final + rcv[c, k].astype(f32)
        out_ref[c * PART : (c + 1) * PART, :] = final.astype(bf16)

    for c in range(CHUNKS):
        for dx in range(NX):
            nx = lax.rem(x + dx, NX)
            if dx == 0:

                @pl.when(jnp.logical_not(here))
                def _():
                    result_copy(c, nx).wait_send()
            else:
                result_copy(c, nx).wait_send()
    for copy in pending + weight_sends + ring_sends + exchange:
        copy.wait_send()
    for k in range(len(SHARED_TO)):
        remote(slot_ref(0), slot_ref(0), key_send.at[60 + k], key_recv.at[0], sibling).wait_send()
    for p in range(32):
        remote(slot_ref(p), slot_ref(p), sib_send.at[p], sib_recv.at[p], sibling).wait_send()


def body(
    query_plain,
    query_rotary,
    latent_cache,
    key_rotary,
    latent_gain,
    positions,
    absorb_keys,
    absorb_values,
    output_weight,
):
    f32, bf16 = jnp.float32, jnp.bfloat16
    frequency = np.tile(rope_base ** (-np.arange(ROPE // 2) / (ROPE // 2)), 4)[None, :]
    inner = np.arange(HALF)[:, None] * frequency
    outer = np.arange(0, 4096, HALF)[:, None] * frequency
    tables = [f(a).astype(np.float32) for a in (outer, inner) for f in (np.cos, np.sin)]
    vmem = pl.BlockSpec(memory_space=pltpu.VMEM)
    hbm = pl.BlockSpec(memory_space=pl.ANY)
    dma = pltpu.SemaphoreType.DMA
    call = pl.pallas_call(
        kernel,
        out_shape=jax.ShapeDtypeStruct((TOK, COLS), bf16),
        in_specs=[hbm] * 13,
        out_specs=vmem,
        scratch_shapes=[
            pltpu.SMEM((TOK,), jnp.int32),
            pltpu.VMEM((ROWS, NOPE), bf16),
            pltpu.VMEM((ROWS, ROPE), bf16),
            pltpu.VMEM((TOK, LAT), bf16),
            pltpu.VMEM((TOK, ROPE), bf16),
            pltpu.VMEM((1, LAT), f32),
            pltpu.VMEM((128, 128), f32),
            pltpu.VMEM((128, 128), f32),
            pltpu.VMEM((HALF, 128), f32),
            pltpu.VMEM((HALF, 128), f32),
            pltpu.VMEM((HEADS, NOPE, LAT), bf16),
            pltpu.VMEM((HEADS, LAT, VD), bf16),
            pltpu.VMEM((8, 8 * HALF, WIDE), bf16),
            pltpu.VMEM((HEADS, TOK, NOPE), bf16),
            pltpu.VMEM((CHUNKS, HEADS, PART, LAT + 256), bf16),
            pltpu.VMEM((2, ROWS, 512), f32),
            pltpu.VMEM((2, ROWS, 128), f32),
            pltpu.VMEM((ROWS, 128), f32),
            pltpu.VMEM((ROWS, 128), f32),
            pltpu.VMEM((ROWS, LAT), f32),
            pltpu.VMEM((8, 8, 2, COLS), bf16),
            pltpu.VMEM((HEADS, VD, COLS), bf16),
            pltpu.VMEM((CHUNKS, NX, PART, HEADS * VD), bf16),
            pltpu.VMEM((CHUNKS, NX, PART, COLS), bf16),
            pltpu.VMEM((CHUNKS, NY, PART, COLS), bf16),
            dma((13,)),
            dma((63,)),
            dma((32,)),
            dma((32,)),
            dma((32,)),
            dma((8,)),
            dma((8,)),
            dma((32,)),
            dma((16,)),
            dma((16,)),
            dma((16,)),
            dma((4 * CHUNKS,)),
            dma((4 * CHUNKS,)),
            dma((NX * CHUNKS,)),
            dma((NY * CHUNKS,)),
        ],
        compiler_params=pltpu.CompilerParams(
            collective_id=0, has_side_effects=True, vmem_limit_bytes=60 * 1024 * 1024
        ),
        cost_estimate=pl.CostEstimate(
            flops=11_000_000_000, bytes_accessed=6_000_000, transcendentals=4_200_000
        ),
    )
    return call(
        positions,
        query_plain.reshape(ROWS, NOPE),
        query_rotary.reshape(ROWS, ROPE),
        latent_cache,
        key_rotary,
        latent_gain.reshape(1, LAT),
        *tables,
        absorb_keys,
        absorb_values,
        output_weight,
    )


def solution(mesh):
    return jax.shard_map(
        body,
        mesh=mesh,
        in_specs=(
            P("ctx", "head", None),
            P("ctx", "head", None),
            P("ctx", None),
            P("ctx", None),
            P(),
            P("ctx"),
            P("head", None, None),
            P("head", None, None),
            P("head", "ctx", None),
        ),
        out_specs=P("ctx", "head"),
        check_vma=False,
    )
```
